256 devices in a mesh: ctx: 16 (over y_lo, x, core), fsdp: 16 (over y_hi, z).
Axes of the slice: x: 4, y: 4 (y_hi: 2, y_lo: 2; y = y_hi * 2 + y_lo), z: 8, core: 2. Of those that a mesh axis runs over, the one named last changes fastest.
Arguments:
- tokens: bfloat16 [4096, 3072], P('ctx'), may hold values from -6 to 6
- cotangent: bfloat16 [4096, 3072], P('ctx'), may hold values from -6 to 6
- w_query: bfloat16 [3072, 2048], P('ctx', 'fsdp'), may hold values from -0.109375 to 0.109375
- w_key: bfloat16 [3072, 2048], P('ctx', 'fsdp'), may hold values from -0.109375 to 0.109375
- w_value: bfloat16 [3072, 2048], P('ctx', 'fsdp'), may hold values from -0.109375 to 0.109375
- w_out: bfloat16 [3072, 2048], P('ctx', 'fsdp'), may hold values from -0.125 to 0.125
- gain_query: float32 [128], replicated, may hold values from 0.8 to 2
- gain_key: float32 [128], replicated, may hold values from 0.8 to 2
- lengths: int32 [1], replicated, may hold values from 2048 to 4096
Outputs:
- attended: bfloat16 [4096, 3072], P('ctx')
- grad_tokens: bfloat16 [4096, 3072], P('ctx')
- grad_w_query: float32 [3072, 2048], P('ctx', 'fsdp')
- grad_w_key: float32 [3072, 2048], P('ctx', 'fsdp')
- grad_w_value: float32 [3072, 2048], P('ctx', 'fsdp')
- grad_w_out: float32 [3072, 2048], P('ctx', 'fsdp')
- grad_gains: float32 [2, 128], replicated
The draws below stay inside these ranges and needn't reach their ends.
All inputs are finite; a program needn't handle non-finite values.
Results may differ from the reference program's by a relative error of at most 0.03.
Values may be sent and summed in bfloat16 or wider, within the bound.
A program may use at most 64 MiB of HBM per device.

```python
import math
import jax
import jax.numpy as jnp
from jax import lax

D = 3072
HD = 128
TOK_DEV = 256
SEQ = 4096
HEADS = 16
N_CTX = 16


def with_spikes(entries, own_key, source, target, blocks, factor):
    owner, partner = [(jnp.arange(entries.shape[position]) // (entries.shape[position] // blocks)).reshape([-1 if axis == position else 1 for axis in range(entries.ndim)]) for position in (source, target)]
    chosen = jax.random.permutation(own_key, blocks)[partner]
    strong = (owner == chosen) | (owner == (partner + blocks // 2) % blocks)
    return jnp.where(strong, factor * entries, entries)


def levels(stream_key, extent, cuts, least, largest):
    def one(dim, blocks):
        draws = jax.random.uniform(jax.random.fold_in(jax.random.fold_in(stream_key, 6), dim), (blocks,), jnp.float32, least / len(cuts), largest / len(cuts))
        return jnp.repeat(jnp.exp(draws), extent[dim] // blocks).reshape((-1,) + (1,) * (len(extent) - dim - 1))

    level = one(*cuts[0])
    for cut in cuts[1:]:
        level = level * one(*cut)
    return level


def noise(own_key, extent, spread, bound, shards=(), held_as=jnp.bfloat16):
    array = jax.random.normal(own_key, extent, jnp.float32) * spread
    if len(shards) > 0:
        array = levels(own_key, extent, shards, -0.22, 0.18) * array
    return jnp.clip(array, min=-bound, max=bound).astype(held_as)


def gaussian_with(stream_key, extent, spread, limit, cuts, heavy, kind=jnp.bfloat16):
    result = spread * jax.random.normal(stream_key, extent, jnp.float32)
    if cuts:
        result = result * levels(stream_key, extent, cuts, -0.22, 0.18)
    return jnp.clip(with_spikes(result, jax.random.fold_in(stream_key, 3), *heavy), -limit, limit).astype(kind)


def setup_inputs(seed: int = 0) -> dict:
    key_of = jax.random.split(jax.random.key(seed), 10)
    return {
        "tokens": gaussian_with(key_of[0], (SEQ, D), 1.0, 6.0, ((0, 16),), (0, 1, 16, 2.0)),
        "cotangent": gaussian_with(key_of[1], (SEQ, D), 1.0, 6.0, ((0, 16),), (0, 1, 16, 2.0)),
        "w_query": noise(key_of[2], (D, HEADS * HD), D ** -0.5, 0.109375, ((0, 16), (1, 16))),
        "w_key": noise(key_of[3], (D, HEADS * HD), D ** -0.5, 0.109375, ((0, 16), (1, 16))),
        "w_value": noise(key_of[4], (D, HEADS * HD), D ** -0.5, 0.109375, ((0, 16), (1, 16))),
        "w_out": noise(key_of[5], (D, HEADS * HD), (HEADS * HD) ** -0.5, 0.125, ((0, 16), (1, 16))),
        "gain_query": jnp.clip(jax.random.uniform(key_of[6], (HD,), jnp.float32, 0.8, 2.0), 0.8, 2.0),
        "gain_key": jnp.clip(jax.random.uniform(key_of[7], (HD,), jnp.float32, 0.8, 2.0), 0.8, 2.0),
        "lengths": jax.random.randint(key_of[8], (1,), TOK_DEV * N_CTX // 2, TOK_DEV * N_CTX + 1).astype(jnp.int32),
    }


EPS = 1e-06

def norm_back(grad_normed, unit, inv_rms, gain):
    scaled = grad_normed * gain
    return inv_rms * (scaled - unit * lax.optimization_barrier(jnp.mean(scaled * unit, -1, keepdims=True)))

def one_head(tokens, cotangent, length, w_cat, w_out, gain_query, gain_key):
    head = w_out.shape[1]
    inv_root = 1.0 / math.sqrt(head)
    projected = jnp.dot(tokens, w_cat, preferred_element_type=jnp.float32)
    queries = projected[:, :head]
    keys_raw = projected[:, head:2 * head]
    values = projected[:, 2 * head:]
    rms_query = lax.rsqrt(lax.optimization_barrier(jnp.mean(queries * queries, -1, keepdims=True)) + EPS)
    rms_key = lax.rsqrt(lax.optimization_barrier(jnp.mean(keys_raw * keys_raw, -1, keepdims=True)) + EPS)
    unit_query = queries * rms_query
    unit_key = keys_raw * rms_key
    query_n = (unit_query * gain_query).astype(jnp.bfloat16)
    key_n = (unit_key * gain_key).astype(jnp.bfloat16)
    value_b = values.astype(jnp.bfloat16)
    scores = jnp.dot(query_n, key_n.T, preferred_element_type=jnp.float32) * inv_root
    positions = jnp.arange(scores.shape[1], dtype=jnp.int32)
    weights = jnp.where((positions < length)[None, :], jnp.exp(scores), 0.0)
    denom = lax.optimization_barrier(jnp.sum(weights, -1))
    numer = jnp.dot(weights.astype(jnp.bfloat16), value_b, preferred_element_type=jnp.float32)
    mixed = (numer / denom[:, None]).astype(jnp.bfloat16)
    attended_term = jnp.dot(mixed, w_out.T, preferred_element_type=jnp.float32)
    grad_mixed = jnp.dot(cotangent, w_out, preferred_element_type=jnp.float32).astype(jnp.bfloat16)
    delta = lax.optimization_barrier(jnp.sum(grad_mixed.astype(jnp.float32) * mixed.astype(jnp.float32), -1))
    probs = weights / denom[:, None]
    grad_probs = jnp.dot(grad_mixed, value_b.T, preferred_element_type=jnp.float32)
    grad_scores = probs * (grad_probs - delta[:, None])
    scores_b = grad_scores.astype(jnp.bfloat16)
    probs_b = probs.astype(jnp.bfloat16)
    grad_qn = jnp.dot(scores_b, key_n, preferred_element_type=jnp.float32) * inv_root
    grad_kn = jnp.dot(scores_b.T, query_n, preferred_element_type=jnp.float32) * inv_root
    grad_value = jnp.dot(probs_b.T, grad_mixed, preferred_element_type=jnp.float32)
    grad_query = norm_back(grad_qn, unit_query, rms_query, gain_query)
    grad_key = norm_back(grad_kn, unit_key, rms_key, gain_key)
    grad_cat = jnp.concatenate([grad_query, grad_key, grad_value], 1).astype(jnp.bfloat16)
    token_term = jnp.dot(grad_cat, w_cat.T, preferred_element_type=jnp.float32)
    weight_terms = jnp.concatenate([jnp.dot(tokens.T, grad_cat, preferred_element_type=jnp.float32), jnp.dot(cotangent.T, mixed, preferred_element_type=jnp.float32)], 1)
    gain_terms = jnp.stack([lax.optimization_barrier(jnp.sum(grad_qn * unit_query, 0)), lax.optimization_barrier(jnp.sum(grad_kn * unit_key, 0))])
    return (attended_term, token_term, weight_terms, gain_terms)

def split_heads(weight, head):
    rows = weight.shape[0]
    return jnp.transpose(weight.reshape(rows, weight.shape[1] // head, head), (1, 0, 2))

def join_heads(stacked):
    return jnp.transpose(stacked, (1, 0, 2)).reshape(stacked.shape[1], stacked.shape[0] * stacked.shape[2])

def reference(tokens, cotangent, w_query, w_key, w_value, w_out, gain_query, gain_key, lengths):
    head = gain_query.shape[0]
    cat_heads = jnp.concatenate([split_heads(w_query, head), split_heads(w_key, head), split_heads(w_value, head)], 2)
    out_heads = split_heads(w_out, head)
    length = lengths[0]

    def visit(carry, inputs):
        attended_term, token_term, weight_terms, gain_terms = one_head(tokens, cotangent, length, inputs[0], inputs[1], gain_query, gain_key)
        return ((carry[0] + attended_term, carry[1] + token_term, carry[2] + gain_terms), weight_terms)
    start = (jnp.zeros(tokens.shape, jnp.float32), jnp.zeros(tokens.shape, jnp.float32), jnp.zeros((2, head), jnp.float32))
    sums, stacked = lax.scan(visit, start, (cat_heads, out_heads))
    attended = sums[0].astype(jnp.bfloat16)
    grad_tokens = sums[1].astype(jnp.bfloat16)
    return (attended, grad_tokens, join_heads(stacked[:, :, :head]), join_heads(stacked[:, :, head:2 * head]), join_heads(stacked[:, :, 2 * head:3 * head]), join_heads(stacked[:, :, 3 * head:]), sums[2])
```

```python
import functools
import math

import jax
import jax.numpy as jnp
from jax import lax
from jax.experimental import pallas as pl
from jax.experimental.pallas import tpu as pltpu
from jax.sharding import PartitionSpec as P

EPS = 1e-06
MESH = pl.DeviceIdType.MESH
BF = jnp.bfloat16
F32 = jnp.float32

TOK = 256
D = 3072
H = 128
WR = 192
NB = 16
NP = 8

OWN, YN, XL, XR, XLY, XRY, OPP, OPPY = range(8)


def nt(a, b):
    return lax.dot_general(a, b, (((1,), (1,)), ((), ())), preferred_element_type=F32)


def tn(a, b):
    return lax.dot_general(a, b, (((0,), (0,)), ((), ())), preferred_element_type=F32)


def nn(a, b):
    return jnp.dot(a, b, preferred_element_type=F32)


class Place:
    def __init__(self):
        c = lax.axis_index("ctx")
        f = lax.axis_index("fsdp")
        self.c, self.f = c, f
        y, x, k = c // 8, (c // 2) % 4, c % 2
        yh, z = f // 8, f % 8
        self.k, self.z = k, z

        def at(y, x, k, yh, z):
            return ((y * 4 + x) * 2 + k, yh * 8 + z)

        xl, xr, xo = (x + 3) % 4, (x + 1) % 4, (x + 2) % 4
        self.sib = at(y, x, 1 - k, yh, z)
        self.xl = at(y, xl, k, yh, z)
        self.xr = at(y, xr, k, yh, z)
        self.xo = at(y, xo, k, yh, z)
        self.x1 = at(y, x + 1 - 2 * (x % 2), k, yh, z)
        self.yn = at(1 - y, x, k, yh, z)
        self.yh = at(y, x, k, 1 - yh, z)
        self.zl = at(y, x, k, yh, (z + 7) % 8)
        self.zr = at(y, x, k, yh, (z + 1) % 8)
        self.z1 = at(y, x, k, yh, z + 1 - 2 * (z % 2))
        self.z2 = at(y, x, k, yh, (z // 4) * 4 + (z + 2) % 4)
        self.z4 = at(y, x, k, yh, (z + 4) % 8)
        self.all = (
            self.sib, self.xl, self.xr, self.xo, self.yn,
            self.yh, self.zl, self.zr, self.z2, self.z4,
        )
        n = 1 - y
        self.chip = (
            y * 4 + x, n * 4 + x, y * 4 + xl, y * 4 + xr,
            n * 4 + xl, n * 4 + xr, y * 4 + xo, n * 4 + xo,
        )


class Link:
    def __init__(self, send, recv):
        self.send, self.recv, self.sent = send, recv, {}

    def start(self, m, src, dst, to):
        copy = pltpu.make_async_remote_copy(
            src_ref=src,
            dst_ref=dst,
            send_sem=self.send.at[m],
            recv_sem=self.recv.at[m],
            device_id=to,
            device_id_type=MESH,
        )
        copy.start()
        self.sent[m] = copy

    def arrived(self, m):
        self.sent[m].wait_recv()

    def drain(self):
        for copy in self.sent.values():
            copy.wait_send()


def gather(pc, full, rows, link):
    def block(t, core, lo=0, n=rows):
        start = pl.multiple_of(pc.chip[t] * (2 * rows) + core * rows + lo, 32)
        return full.at[pl.ds(start, n), :]

    half = rows // 2

    def push(m, t, to, lo=0, n=rows):
        ref = block(t, pc.k, lo, n)
        link.start(m, ref, ref, to)

    def share(t):
        push(8 + t, t, pc.sib)

    push(0, OWN, pc.yn)
    push(1, OWN, pc.xl)
    push(2, OWN, pc.xr)
    share(OWN)
    yield None
    link.arrived(0)
    push(3, YN, pc.xl)
    push(4, YN, pc.xr)
    share(YN)
    link.arrived(8 + OWN)
    yield OWN
    link.arrived(1)
    push(6, XR, pc.xl, half, half)
    share(XR)
    link.arrived(2)
    push(5, XL, pc.xr, 0, half)
    share(XL)
    link.arrived(8 + YN)
    yield YN
    link.arrived(8 + XR)
    yield XR
    link.arrived(8 + XL)
    yield XL
    link.arrived(3)
    share(XRY)
    link.arrived(4)
    share(XLY)
    link.arrived(5)
    link.arrived(6)
    push(7, OPP, pc.yn)
    share(OPP)
    link.arrived(8 + XRY)
    yield XRY
    link.arrived(8 + XLY)
    yield XLY
    link.arrived(8 + OPP)
    yield OPP
    link.arrived(7)
    share(OPPY)
    link.arrived(8 + OPPY)
    yield OPPY
    link.drain()


ORDER = (OPPY, OPP, XLY, XRY, XL, XR, YN, OWN)


def scatter(pc, make, part, own, rows, link, sbuf, rbuf):
    half = rows // 2
    mine = pl.multiple_of(pc.k * rows, rows)
    theirs = pl.multiple_of((1 - pc.k) * rows, rows)

    for t in ORDER:
        make(t)
        sbuf[8 + t] = part[t, pl.ds(theirs, rows), :].astype(BF)
        link.start(8 + t, sbuf.at[8 + t], rbuf.at[8 + t], pc.sib)
        yield "made"

    def chip_sum(t):
        link.arrived(8 + t)
        return part[t, pl.ds(mine, rows), :] + rbuf[8 + t].astype(F32)

    def got(m):
        link.arrived(m)
        return rbuf[m].astype(F32)

    def push(m, value, to):
        sbuf[m] = value.astype(BF)
        link.start(m, sbuf.at[m], rbuf.at[m], to)

    push(0, chip_sum(OPPY), pc.yn)
    push(1, chip_sum(XLY), pc.xl)
    push(2, chip_sum(XRY), pc.xr)
    yield "a"
    total = chip_sum(OPP) + got(0)
    sbuf[3] = total.astype(BF)
    lo, hi = pl.ds(0, half), pl.ds(half, half)
    link.start(3, sbuf.at[3, lo], rbuf.at[3, lo], pc.xl)
    link.start(4, sbuf.at[3, hi], rbuf.at[3, hi], pc.xr)
    yield "b"
    link.arrived(3)
    near = chip_sum(XL)
    sbuf[5, lo] = (near[:half] + rbuf[3, lo].astype(F32)).astype(BF)
    sbuf[5, hi] = near[half:].astype(BF)
    link.start(5, sbuf.at[5], rbuf.at[5], pc.xl)
    link.arrived(4)
    near = chip_sum(XR)
    sbuf[6, lo] = near[:half].astype(BF)
    sbuf[6, hi] = (near[half:] + rbuf[3, hi].astype(F32)).astype(BF)
    link.start(6, sbuf.at[6], rbuf.at[6], pc.xr)
    yield "c"
    push(7, chip_sum(YN) + got(1) + got(2), pc.yn)
    yield "d"
    own[...] = chip_sum(OWN) + got(5) + got(6) + got(7)
    link.drain()


SUB = 16

RIGHT = ((4, 0), (3, 1), (3, 0), (2, 1), (2, 0), (1, 1), (1, 0))
LEFT = ((4, 1), (3, 0), (3, 1), (2, 0), (2, 1), (1, 0), (1, 1))


def sum_heads(pc, term, out, link, sbuf, rbuf):
    def rows(chip, u):
        return pl.ds(pl.multiple_of(chip * (2 * SUB) + u * SUB, SUB), SUB)

    def owner(distance):
        return (pc.z + 8 + distance) % 8

    right = {m: i for i, m in enumerate(RIGHT)}
    left = {m: 7 + i for i, m in enumerate(LEFT)}
    for i in range(7):
        for side, sign, steps, to in ((right, 1, RIGHT, pc.zr), (left, -1, LEFT, pc.zl)):
            d, u = steps[i]
            value = term[rows(owner(sign * d), u), :]
            before = side.get((d + 1, u))
            if before is not None:
                link.arrived(before)
                value = value + rbuf[before].astype(F32)
            m = side[(d, u)]
            sbuf[m] = value.astype(BF)
            link.start(m, sbuf.at[m], rbuf.at[m], to)
        yield "reduce"
    for u in (0, 1):
        value = term[rows(pc.z, u), :]
        for m in (right[(1, u)], left[(1, u)]):
            link.arrived(m)
            value = value + rbuf[m].astype(F32)
        sbuf[14 + u] = value.astype(BF)
        link.start(14 + u, sbuf.at[14 + u], rbuf.at[14 + u], pc.yh)
        yield "reduced"

    def forward(m, chip, u, to):
        ref = out.at[rows(chip, u), :]
        link.start(m, ref, ref, to)

    for u in (0, 1):
        link.arrived(14 + u)
        total = sbuf[14 + u].astype(F32) + rbuf[14 + u].astype(F32)
        out[rows(pc.z, u), :] = total.astype(BF)
        forward(16 + u, pc.z, u, pc.zr)
        forward(23 + u, pc.z, u, pc.zl)
        yield "exchanged"
    for hop in (1, 2, 3):
        for u in (0, 1):
            if hop < 3 or u == 0:
                link.arrived(16 + 2 * (hop - 1) + u)
                forward(16 + 2 * hop + u if hop < 3 else 22, owner(-hop), u, pc.zr)
            if hop < 3 or u == 1:
                link.arrived(23 + 2 * (hop - 1) + u)
                forward(23 + 2 * hop + u if hop < 3 else 29, owner(hop), u, pc.zl)
            yield "gather"
    link.arrived(16 + 5)
    link.arrived(23 + 4)
    link.arrived(22)
    link.arrived(29)
    link.drain()


def sum_small(pc, value_ref, link, rbuf):
    for m, to in enumerate((pc.sib, pc.x1, pc.xo, pc.yn, pc.z1, pc.z2, pc.z4, pc.yh)):
        link.start(m, value_ref.at[m], rbuf.at[m], to)
        yield "sent"
        link.arrived(m)
        value_ref[m + 1] = value_ref[m] + rbuf[m]
    link.drain()


def inv_rms(values):
    return lax.rsqrt(jnp.mean(values * values, -1, keepdims=True) + EPS)


def norm_back(grad, unit, rms, gain):
    scaled = grad * gain
    return rms * (scaled - unit * jnp.mean(scaled * unit, -1, keepdims=True))


def kernel(
    length_ref, tokens, cotangent, w_query, w_key, w_value, w_out, gain_query, gain_key,
    attended, grad_tokens, g_query, g_key, g_value, g_out, g_gains,
    wfull, proj, gacc, kvfull, qn, gb, mixed, dc, probs, gprobs, oacc, qacc, dkv, dkv_own, term, wpart, w_own,
    gain_v, gain_r, s_dkv, r_dkv, s_w, r_w, s_att, r_att, s_tok, r_tok,
    sw, rw, skv, rkv, sdk, rdk, sdw, rdw, sat, rat, stk, rtk, sgn, rgn,
):
    pc = Place()
    inv_root = 1.0 / math.sqrt(H)
    length = length_ref[0]

    barrier = pltpu.get_barrier_semaphore()
    for other in pc.all:
        pl.semaphore_signal(barrier, inc=1, device_id=other, device_id_type=MESH)

    own_rows = pl.ds(pl.multiple_of(pc.c * WR, WR), WR)
    for i, w in enumerate((w_query, w_key, w_value, w_out)):
        wfull[own_rows, i * H : (i + 1) * H] = w[...]
    proj[...] = jnp.zeros_like(proj)
    gacc[...] = jnp.zeros_like(gacc)
    oacc[...] = jnp.zeros_like(oacc)
    qacc[...] = jnp.zeros_like(qacc)
    gain_v[...] = jnp.zeros_like(gain_v)
    pl.semaphore_wait(barrier, len(pc.all))

    def model_rows(t):
        return pl.ds(pl.multiple_of(pc.chip[t] * (2 * WR), 2 * WR), 2 * WR)

    def key_rows(t):
        return pl.ds(pl.multiple_of(pc.chip[t] * (2 * TOK), 2 * TOK), 2 * TOK)

    for t in gather(pc, wfull, WR, Link(sw, rw)):
        if t is not None:
            r = model_rows(t)
            proj[...] += nn(tokens[:, r], wfull[r, 0 : 3 * H])
            gacc[...] += nn(cotangent[:, r], wfull[r, 3 * H : 4 * H])

    def unit_of(i):
        values = proj[:, i * H : (i + 1) * H]
        rms = inv_rms(values)
        return values * rms, rms

    gain_q, gain_k = gain_query[...], gain_key[...]
    own_keys = pl.ds(pl.multiple_of(pc.c * TOK, TOK), TOK)
    kvfull[own_keys, 0:H] = (unit_of(1)[0] * gain_k).astype(BF)
    kvfull[own_keys, H : 2 * H] = proj[:, 2 * H : 3 * H].astype(BF)

    denom = jnp.zeros((1, TOK), F32)
    for t in gather(pc, kvfull, TOK, Link(skv, rkv)):
        if t is None:
            qn[...] = (unit_of(0)[0] * gain_q).astype(BF)
            gb[...] = gacc[...].astype(BF)
            continue
        keys, values = kvfull[key_rows(t), 0:H], kvfull[key_rows(t), H : 2 * H]
        scores = nt(keys, qn[...]) * inv_root
        place = pc.chip[t] * (2 * TOK) + lax.broadcasted_iota(jnp.int32, scores.shape, 0)
        weights = jnp.where(place < length, jnp.exp(scores), 0.0)
        probs[t] = weights
        denom = denom + jnp.sum(weights, 0, keepdims=True)
        oacc[...] += tn(values, weights.astype(BF))
        gprobs[t] = nt(values, gb[...])

    inv_denom = 1.0 / denom
    mixed_t = oacc[...] / denom
    mixed[...] = mixed_t.T.astype(BF)
    delta = jnp.sum(gb[...].astype(F32).T * mixed_t.astype(BF).astype(F32), 0, keepdims=True)

    term[0] = nt(mixed[...], wfull[:, 3 * H : 4 * H])
    att = sum_heads(pc, term.at[0], attended, Link(sat, rat), s_att, r_att)
    next(att)

    def keys_back(t):
        keys = kvfull[key_rows(t), 0:H]
        probs_t = probs[t] * inv_denom
        scores_b = (probs_t * (gprobs[t] - delta)).astype(BF)
        qacc[...] += tn(keys, scores_b)
        dkv[t, :, 0:H] = nn(scores_b, qn[...]) * inv_root
        dkv[t, :, H : 2 * H] = nn(probs_t.astype(BF), gb[...])

    def step(work, n=1):
        for _ in range(n):
            next(work, None)

    made = 0
    for mark in scatter(pc, keys_back, dkv, dkv_own, TOK, Link(sdk, rdk), s_dkv, r_dkv):
        made += 1
        if mark != "made" or made % 3 == 0:
            step(att)

    grad_qn = qacc[...].T * inv_root
    grad_kn = dkv_own[:, 0:H]
    unit_q, rms_q = unit_of(0)
    unit_k, rms_k = unit_of(1)
    dc[:, 0:H] = norm_back(grad_qn, unit_q, rms_q, gain_q).astype(BF)
    dc[:, H : 2 * H] = norm_back(grad_kn, unit_k, rms_k, gain_k).astype(BF)
    dc[:, 2 * H : 3 * H] = dkv_own[:, H : 2 * H].astype(BF)

    term[1] = nt(dc[...], wfull[:, 0 : 3 * H])
    tok = sum_heads(pc, term.at[1], grad_tokens, Link(stk, rtk), s_tok, r_tok)
    next(tok)

    gain_v[0, 0:1, :] = jnp.sum(grad_qn * unit_q, 0, keepdims=True)
    gain_v[0, 1:2, :] = jnp.sum(grad_kn * unit_k, 0, keepdims=True)
    gains = sum_small(pc, gain_v, Link(sgn, rgn), gain_r)

    def weights_back(t):
        r = model_rows(t)
        wpart[t, :, 0 : 3 * H] = tn(tokens[:, r], dc[...])
        wpart[t, :, 3 * H : 4 * H] = tn(cotangent[:, r], mixed[...])

    made = 0
    for mark in scatter(pc, weights_back, wpart, w_own, WR, Link(sdw, rdw), s_w, r_w):
        made += 1
        if mark != "made" or made % 2 == 0:
            step(tok)
            step(att)
            step(gains)
    for i, g in enumerate((g_query, g_key, g_value, g_out)):
        g[...] = w_own[:, i * H : (i + 1) * H]
    for _ in range(20):
        step(att)
        step(tok)
        step(gains)
    g_gains[...] = gain_v[8, 0:2, :]


def on_device(tokens, cotangent, w_query, w_key, w_value, w_out, gain_query, gain_key, lengths):
    vmem = pl.BlockSpec(memory_space=pltpu.VMEM)
    smem = pl.BlockSpec(memory_space=pltpu.SMEM)
    shape = jax.ShapeDtypeStruct
    dma = pltpu.SemaphoreType.DMA
    out = pl.pallas_call(
        kernel,
        name="sublayer",
        out_shape=[
            shape((TOK, D), BF),
            shape((TOK, D), BF),
            *[shape((WR, H), F32)] * 4,
            shape((2, H), F32),
        ],
        in_specs=[smem] + [vmem] * 8,
        out_specs=[vmem] * 7,
        scratch_shapes=[
            pltpu.VMEM((D, 4 * H), BF),
            pltpu.VMEM((TOK, 3 * H), F32),
            pltpu.VMEM((TOK, H), F32),
            pltpu.VMEM((NB * TOK, 2 * H), BF),
            pltpu.VMEM((TOK, H), BF),
            pltpu.VMEM((TOK, H), BF),
            pltpu.VMEM((TOK, H), BF),
            pltpu.VMEM((TOK, 3 * H), BF),
            pltpu.VMEM((NP, 2 * TOK, TOK), F32),
            pltpu.VMEM((NP, 2 * TOK, TOK), F32),
            pltpu.VMEM((H, TOK), F32),
            pltpu.VMEM((H, TOK), F32),
            pltpu.VMEM((NP, 2 * TOK, 2 * H), F32),
            pltpu.VMEM((TOK, 2 * H), F32),
            pltpu.VMEM((2, TOK, D), F32),
            pltpu.VMEM((NP, 2 * WR, 4 * H), F32),
            pltpu.VMEM((WR, 4 * H), F32),
            pltpu.VMEM((9, 8, H), F32),
            pltpu.VMEM((8, 8, H), F32),
            pltpu.VMEM((16, TOK, 2 * H), BF),
            pltpu.VMEM((16, TOK, 2 * H), BF),
            pltpu.VMEM((16, WR, 4 * H), BF),
            pltpu.VMEM((16, WR, 4 * H), BF),
            *[pltpu.VMEM((16, SUB, D), BF)] * 4,
            *[dma((16,))] * 8,
            *[dma((30,))] * 4,
            *[dma((8,))] * 2,
        ],
        compiler_params=pltpu.CompilerParams(
            collective_id=0, has_side_effects=True, vmem_limit_bytes=60 * 2**20
        ),
        cost_estimate=pl.CostEstimate(flops=9 * 10**9, bytes_accessed=8 * 2**20, transcendentals=10**6),
    )(
        lengths, tokens, cotangent, w_query, w_key, w_value, w_out,
        gain_query.reshape(1, H), gain_key.reshape(1, H),
    )
    return tuple(out)


def solution(mesh):
    placed = (
        P("ctx", None),
        P("ctx", None),
        P("ctx", "fsdp"),
        P("ctx", "fsdp"),
        P("ctx", "fsdp"),
        P("ctx", "fsdp"),
        P(),
        P(),
        P(),
    )
    return jax.shard_map(
        on_device,
        mesh=mesh,
        in_specs=placed,
        out_specs=(
            P("ctx", None),
            P("ctx", None),
            P("ctx", "fsdp"),
            P("ctx", "fsdp"),
            P("ctx", "fsdp"),
            P("ctx", "fsdp"),
            P(),
        ),
        check_vma=False,
    )
```

```python
import functools
import math

import jax
import jax.numpy as jnp
from jax import lax
from jax.experimental import pallas as pl
from jax.experimental.pallas import tpu as pltpu
from jax.sharding import PartitionSpec as P

EPS = 1e-06
MESH = pl.DeviceIdType.MESH
BF = jnp.bfloat16
F32 = jnp.float32

TOK = 256
D = 3072
H = 128
WR = 192
NB = 16
NP = 8

OWN, YN, XL, XR, XLY, XRY, OPP, OPPY = range(8)


def nt(a, b):
    return lax.dot_general(a, b, (((1,), (1,)), ((), ())), preferred_element_type=F32)


def tn(a, b):
    return lax.dot_general(a, b, (((0,), (0,)), ((), ())), preferred_element_type=F32)


def nn(a, b):
    return jnp.dot(a, b, preferred_element_type=F32)


class Place:
    def __init__(self):
        c = lax.axis_index("ctx")
        f = lax.axis_index("fsdp")
        self.c, self.f = c, f
        y, x, k = c // 8, (c // 2) % 4, c % 2
        yh, z = f // 8, f % 8
        self.k, self.z, self.y_hi = k, z, yh

        def at(y, x, k, yh, z):
            return ((y * 4 + x) * 2 + k, yh * 8 + z)

        xl, xr, xo = (x + 3) % 4, (x + 1) % 4, (x + 2) % 4
        self.sib = at(y, x, 1 - k, yh, z)
        self.xl = at(y, xl, k, yh, z)
        self.xr = at(y, xr, k, yh, z)
        self.xo = at(y, xo, k, yh, z)
        self.x1 = at(y, x + 1 - 2 * (x % 2), k, yh, z)
        self.yn = at(1 - y, x, k, yh, z)
        self.yh = at(y, x, k, 1 - yh, z)
        self.zl = at(y, x, k, yh, (z + 7) % 8)
        self.zr = at(y, x, k, yh, (z + 1) % 8)
        self.z1 = at(y, x, k, yh, z + 1 - 2 * (z % 2))
        self.z2 = at(y, x, k, yh, (z // 4) * 4 + (z + 2) % 4)
        self.z4 = at(y, x, k, yh, (z + 4) % 8)
        self.all = (
            self.sib, self.xl, self.xr, self.xo, self.yn,
            self.yh, self.zl, self.zr, self.z2, self.z4,
        )
        n = 1 - y
        self.chip = (
            y * 4 + x, n * 4 + x, y * 4 + xl, y * 4 + xr,
            n * 4 + xl, n * 4 + xr, y * 4 + xo, n * 4 + xo,
        )


class Link:
    def __init__(self, send, recv):
        self.send, self.recv, self.sent = send, recv, {}

    def copy(self, m, src, dst, to):
        return pltpu.make_async_remote_copy(
            src_ref=src,
            dst_ref=dst,
            send_sem=self.send,
            recv_sem=self.recv.at[m],
            device_id=to,
            device_id_type=MESH,
        )

    def start(self, m, src, dst, to):
        self.sent[m] = self.copy(m, src, dst, to)
        self.sent[m].start()

    def arrived(self, m):
        self.sent[m].wait_recv()

    def drain(self, sized, to):
        self.copy(0, sized, sized, to).wait_send()


def gather(pc, full, rows, link):
    half = rows // 2
    lo, hi = (0, half), (half, half)
    whole = (0, rows)

    def push(m, t, to, part=whole):
        start = pl.multiple_of(pc.chip[t] * (2 * rows) + pc.k * rows + part[0], 16)
        ref = full.at[pl.ds(start, part[1]), :]
        link.start(m, ref, ref, to)

    def share(t):
        push(11 + t, t, pc.sib)

    push(0, OWN, pc.yn)
    push(1, OWN, pc.xl, hi)
    push(2, OWN, pc.xr, lo)
    push(3, OWN, pc.xl, lo)
    push(4, OWN, pc.xr, hi)
    share(OWN)
    yield ()
    link.arrived(1)
    push(7, XR, pc.xl, hi)
    link.arrived(2)
    push(8, XL, pc.xr, lo)
    yield ()
    link.arrived(0)
    push(5, YN, pc.xl)
    push(6, YN, pc.xr)
    share(YN)
    link.arrived(11 + OWN)
    yield (OWN,)
    link.arrived(3)
    share(XR)
    link.arrived(4)
    share(XL)
    link.arrived(11 + YN)
    yield (YN,)
    link.arrived(8)
    push(9, OPP, pc.yn, lo)
    link.arrived(7)
    push(10, OPP, pc.yn, hi)
    share(OPP)
    link.arrived(11 + XR)
    link.arrived(11 + XL)
    yield (XR, XL)
    link.arrived(5)
    share(XRY)
    link.arrived(6)
    share(XLY)
    link.arrived(11 + OPP)
    yield (OPP,)
    link.arrived(9)
    push(18, OPPY, pc.sib, lo)
    link.arrived(10)
    push(19, OPPY, pc.sib, hi)
    link.arrived(11 + XRY)
    link.arrived(11 + XLY)
    yield (XRY, XLY)
    link.arrived(18)
    link.arrived(19)
    yield (OPPY,)
    link.drain(full.at[pl.ds(0, 15 * rows), :], pc.sib)


def scatter(pc, make, part, own, rows, link, sbuf, rbuf):
    half = rows // 2
    lo, hi, whole = pl.ds(0, half), pl.ds(half, half), pl.ds(0, rows)
    mine = pl.multiple_of(pc.k * rows, rows)
    theirs = pl.multiple_of((1 - pc.k) * rows, rows)

    def made(t):
        make(t)
        sbuf[8 + t] = part[t, pl.ds(theirs, rows), :].astype(BF)
        link.start(11 + t, sbuf.at[8 + t], rbuf.at[8 + t], pc.sib)

    def chip_sum(t):
        link.arrived(11 + t)
        part[t, pl.ds(mine, rows), :] += rbuf[8 + t].astype(F32)

    def add(t, slot, m, rows_of=whole):
        link.arrived(m)
        span = pl.ds(pl.multiple_of(mine + rows_of.start, half), rows_of.size)
        part[t, span, :] += rbuf[slot, rows_of, :].astype(F32)

    def push(m, t, slot, to, rows_of=whole):
        span = pl.ds(pl.multiple_of(mine + rows_of.start, half), rows_of.size)
        sbuf[slot, rows_of, :] = part[t, span, :].astype(BF)
        link.start(m, sbuf.at[slot, rows_of], rbuf.at[slot, rows_of], to)

    made(OPPY)
    made(OPP)
    chip_sum(OPPY)
    push(0, OPPY, 0, pc.yn, lo)
    push(1, OPPY, 0, pc.yn, hi)
    yield
    made(XLY)
    made(XRY)
    chip_sum(XLY)
    push(2, XLY, 1, pc.xl)
    chip_sum(XRY)
    push(3, XRY, 2, pc.xr)
    yield
    made(XL)
    made(XR)
    chip_sum(OPP)
    add(OPP, 0, 0, lo)
    push(4, OPP, 3, pc.xl, lo)
    add(OPP, 0, 1, hi)
    push(5, OPP, 3, pc.xr, hi)
    yield
    chip_sum(XL)
    push(6, XL, 5, pc.xl, hi)
    chip_sum(XR)
    push(7, XR, 6, pc.xr, lo)
    made(YN)
    made(OWN)
    yield
    chip_sum(YN)
    add(XL, 3, 4, lo)
    push(8, XL, 5, pc.xl, lo)
    add(XR, 3, 5, hi)
    push(9, XR, 6, pc.xr, hi)
    yield
    add(YN, 1, 2)
    add(YN, 2, 3)
    push(10, YN, 7, pc.yn)
    yield
    chip_sum(OWN)
    for m in (6, 7, 8, 9, 10):
        link.arrived(m)
    own[...] = part[OWN, pl.ds(mine, rows), :] + (
        rbuf[5].astype(F32) + rbuf[6].astype(F32) + rbuf[7].astype(F32)
    )
    yield
    link.drain(sbuf.at[pl.ds(0, 15)], pc.sib)


SUB = 16
ATT = (((0, D), False),)
TOKENS = (((0, D), False),)

RIGHT = ((4, 0), (3, 1), (3, 0), (2, 1), (2, 0), (1, 1), (1, 0))
LEFT = ((4, 1), (3, 0), (3, 1), (2, 0), (2, 1), (1, 0), (1, 1))


def sum_heads(pc, cols, halves, term, out, link, sbuf, rbuf):
    first, width = cols
    half = width // 2
    full = pl.ds(first, width)

    def at(chip, u):
        return pl.ds(pl.multiple_of(chip * (2 * SUB) + u * SUB, SUB), SUB), full

    def piece(chip, u):
        if not halves:
            return at(chip, u)
        start = pl.multiple_of(chip * (2 * SUB) + pc.y_hi * SUB, SUB)
        return pl.ds(start, SUB), pl.ds(first + u * half, half)

    def owner(distance):
        return (pc.z + 8 + distance) % 8

    right = {m: i for i, m in enumerate(RIGHT)}
    left = {m: 7 + i for i, m in enumerate(LEFT)}
    for i in range(7):
        for side, sign, steps, to in ((right, 1, RIGHT, pc.zr), (left, -1, LEFT, pc.zl)):
            d, u = steps[i]
            value = term[at(owner(sign * d), u)]
            before = side.get((d + 1, u))
            if before is not None:
                link.arrived(before)
                value = value + rbuf[before].astype(F32)
            m = side[(d, u)]
            sbuf[m] = value.astype(BF)
            link.start(m, sbuf.at[m], rbuf.at[m], to)
        yield

    def total(u):
        value = term[at(pc.z, u)]
        for m in (right[(1, u)], left[(1, u)]):
            link.arrived(m)
            value = value + rbuf[m].astype(F32)
        return value.astype(BF)

    def forward(m, chip, u, to):
        ref = out.at[piece(chip, u)]
        link.start(m, ref, ref, to)

    def spread(u):
        forward(16 + u, pc.z, u, pc.zr)
        forward(23 + u, pc.z, u, pc.zl)
        if halves:
            forward(30 + u, pc.z, u, pc.yh)

    for u in (0, 1):
        sbuf[14 + u] = total(u)
        if not halves:
            link.start(14 + u, sbuf.at[14 + u], rbuf.at[14 + u], pc.yh)
        elif u == 1:
            link.start(14, sbuf.at[14 + 1 - pc.y_hi], rbuf.at[14], pc.yh)
        yield
    for u in (0, 1):
        if not halves:
            link.arrived(14 + u)
            both = sbuf[14 + u].astype(F32) + rbuf[14 + u].astype(F32)
            out[at(pc.z, u)] = both.astype(BF)
        elif u == 0:
            link.arrived(14)
            both = sbuf[14 + pc.y_hi].astype(F32) + rbuf[14].astype(F32)
            out[at(pc.z, pc.y_hi)] = both.astype(BF)
        spread(u)
        yield

    def hop_id(base, hop, u):
        return base + (2 * (hop - 1) + u if hop < 4 else 6)

    extra = 32
    for hop in (1, 2, 3, 4):
        for u in (0, 1):
            for base, sign, to, last in ((16, -1, pc.zr, 0), (23, 1, pc.zl, 1)):
                if hop == 4 and u != last:
                    continue
                link.arrived(hop_id(base, hop, u))
                if hop < 3 or (hop == 3 and u == last):
                    forward(hop_id(base, hop + 1, u), owner(sign * hop), u, to)
                if halves:
                    forward(extra, owner(sign * hop), u, pc.yh)
                    extra += 1
            yield
    if halves:
        for m in range(30, extra):
            link.arrived(m)
    link.drain(term.at[pl.ds(0, 15 * SUB), full], pc.zr)


def sum_small(pc, value_ref, link, rbuf):
    for m, to in enumerate((pc.sib, pc.x1, pc.xo, pc.yn, pc.z1, pc.z2, pc.z4, pc.yh)):
        link.start(m, value_ref.at[m], rbuf.at[m], to)
        yield "sent"
        link.arrived(m)
        value_ref[m + 1] = value_ref[m] + rbuf[m]
    link.drain(value_ref.at[pl.ds(0, 8)], pc.sib)


def inv_rms(values):
    return lax.rsqrt(jnp.mean(values * values, -1, keepdims=True) + EPS)


def norm_back(grad, unit, rms, gain):
    scaled = grad * gain
    return rms * (scaled - unit * jnp.mean(scaled * unit, -1, keepdims=True))


def kernel(
    length_ref, tokens_in, cotangent_in, w_query, w_key, w_value, w_out, gain_query, gain_key,
    attended, grad_tokens, g_query, g_key, g_value, g_out, g_gains,
    tokens, cotangent, wkv, wqo, kvp, qp, gacc, kvfull, qn, gb, mixed, dc, probs, gprobs, oacc, qacc,
    dkv, dkv_own, term, wpart, w_own, att_v, tok_v,
    gain_v, gain_r, s_dkv, r_dkv, s_w, r_w, *rest,
):
    lanes = [(rest[2 * i], rest[2 * i + 1]) for i in range(len(ATT) + len(TOKENS))]
    sent, r_kv, r_qo, r_keys, r_gain, local, *r_lanes = rest[2 * len(lanes) :]
    pc = Place()
    inv_root = 1.0 / math.sqrt(H)
    length = length_ref[0]

    barrier = pltpu.get_barrier_semaphore()
    for other in pc.all:
        pl.semaphore_signal(barrier, inc=1, device_id=other, device_id_type=MESH)
    load_t = pltpu.make_async_copy(tokens_in, tokens, local.at[0])
    load_t.start()
    load_c = pltpu.make_async_copy(cotangent_in, cotangent, local.at[1])
    load_c.start()

    own_rows = pl.ds(pl.multiple_of(pc.c * WR, WR), WR)
    for full, left, right in ((wkv, w_key, w_value), (wqo, w_query, w_out)):
        full[own_rows, 0:H] = left[...]
        full[own_rows, H : 2 * H] = right[...]
    for total in (kvp, qp, gacc, oacc, qacc, gain_v):
        total[...] = jnp.zeros_like(total)
    pl.semaphore_wait(barrier, len(pc.all))

    def model_rows(t):
        return pl.ds(pl.multiple_of(pc.chip[t] * (2 * WR), 2 * WR), 2 * WR)

    def key_rows(t):
        return pl.ds(pl.multiple_of(pc.chip[t] * (2 * TOK), 2 * TOK), 2 * TOK)

    def unit_of(values):
        rms = inv_rms(values)
        return values * rms, rms

    def step(work, n=1):
        for _ in range(n):
            next(work, None)

    def each(works):
        for work in works:
            step(work)

    def project_kv(chips):
        for t in chips:
            r = model_rows(t)
            kvp[...] += nn(tokens[:, r], wkv[r, :])

    def project_qo(chips):
        for t in chips:
            r = model_rows(t)
            qp[...] += nn(tokens[:, r], wqo[r, 0:H])
            gacc[...] += nn(cotangent[:, r], wqo[r, H : 2 * H])

    def run(work, use, n):
        for _ in range(n):
            use(next(work, ()))

    gain_q, gain_k = gain_query[...], gain_key[...]
    first = gather(pc, wkv, WR, Link(sent.at[0], r_kv))
    second = gather(pc, wqo, WR, Link(sent.at[1], r_qo))
    step(first, 2)
    load_t.wait()
    load_c.wait()
    run(first, project_kv, 3)
    step(second)
    run(first, project_kv, 1)
    step(second)
    run(second, project_qo, 1)
    run(first, project_kv, 2)
    run(second, project_qo, 1)
    own_keys = pl.ds(pl.multiple_of(pc.c * TOK, TOK), TOK)
    kvfull[own_keys, 0:H] = (unit_of(kvp[:, 0:H])[0] * gain_k).astype(BF)
    kvfull[own_keys, H : 2 * H] = kvp[:, H : 2 * H].astype(BF)
    third = gather(pc, kvfull, TOK, Link(sent.at[2], r_keys))
    step(third)
    run(second, project_qo, 2)
    step(third)
    run(second, project_qo, 2)
    step(first)
    step(second)
    qn[...] = (unit_of(qp[...])[0] * gain_q).astype(BF)
    gb[...] = gacc[...].astype(BF)

    denom = jnp.zeros((1, TOK), F32)
    for chips in third:
        for t in chips:
            keys, values = kvfull[key_rows(t), 0:H], kvfull[key_rows(t), H : 2 * H]
            scores = nt(keys, qn[...]) * inv_root
            place = pc.chip[t] * (2 * TOK) + lax.broadcasted_iota(jnp.int32, scores.shape, 0)
            weights = jnp.where(place < length, jnp.exp(scores), 0.0)
            probs[t] = weights
            denom = denom + jnp.sum(weights, 0, keepdims=True)
            oacc[...] += tn(values, weights.astype(BF))
            gprobs[t] = nt(values, gb[...])

    inv_denom = 1.0 / denom
    mixed_t = oacc[...] / denom
    mixed[...] = mixed_t.T.astype(BF)
    delta = jnp.sum(gb[...].astype(F32).T * mixed_t.astype(BF).astype(F32), 0, keepdims=True)

    term[0] = nt(mixed[...], wqo[:, H : 2 * H])
    def sums(config, start, src, dst):
        return [
            sum_heads(pc, *config[i], src, dst, Link(sent.at[6 + n], r_lanes[n]), *lanes[n])
            for i, n in enumerate(range(start, start + len(config)))
        ]

    att = sums(ATT, 0, term.at[0], att_v)
    each(att)

    def keys_back(t):
        keys = kvfull[key_rows(t), 0:H]
        probs_t = probs[t] * inv_denom
        scores_b = (probs_t * (gprobs[t] - delta)).astype(BF)
        qacc[...] += tn(keys, scores_b)
        dkv[t, :, 0:H] = nn(scores_b, qn[...]) * inv_root
        dkv[t, :, H : 2 * H] = nn(probs_t.astype(BF), gb[...])

    for _ in scatter(pc, keys_back, dkv, dkv_own, TOK, Link(sent.at[3], r_kv), s_dkv, r_dkv):
        each(att)

    grad_qn = qacc[...].T * inv_root
    grad_kn = dkv_own[:, 0:H]
    unit_q, rms_q = unit_of(qp[...])
    unit_k, rms_k = unit_of(kvp[:, 0:H])
    dc[:, 0:H] = norm_back(grad_qn, unit_q, rms_q, gain_q).astype(BF)
    dc[:, H : 2 * H] = norm_back(grad_kn, unit_k, rms_k, gain_k).astype(BF)
    dc[:, 2 * H : 3 * H] = dkv_own[:, H : 2 * H].astype(BF)

    term[1] = nt(dc[:, 0:H], wqo[:, 0:H]) + nt(dc[:, H : 3 * H], wkv[...])
    tok = sums(TOKENS, len(ATT), term.at[1], tok_v)
    each(tok)

    gain_v[0, 0:1, :] = jnp.sum(grad_qn * unit_q, 0, keepdims=True)
    gain_v[0, 1:2, :] = jnp.sum(grad_kn * unit_k, 0, keepdims=True)
    gains = sum_small(pc, gain_v, Link(sent.at[5], r_gain), gain_r)

    def weights_back(t):
        r = model_rows(t)
        wpart[t, :, 0 : 3 * H] = tn(tokens[:, r], dc[...])
        wpart[t, :, 3 * H : 4 * H] = tn(cotangent[:, r], mixed[...])

    for i, _ in enumerate(scatter(pc, weights_back, wpart, w_own, WR, Link(sent.at[4], r_qo), s_w, r_w)):
        each(tok)
        step(gains)
        if i < 1:
            each(att)
    for i, g in enumerate((g_query, g_key, g_value, g_out)):
        g[...] = w_own[:, i * H : (i + 1) * H]
    each(tok)
    for _ in range(4):
        each(att)
    step(gains)
    for i in range(12):
        each(tok)
        each(att)
        step(gains)
        if i == 8:
            save_a = pltpu.make_async_copy(att_v, attended, local.at[0])
            save_a.start()
    g_gains[...] = gain_v[8, 0:2, :]
    save_t = pltpu.make_async_copy(tok_v, grad_tokens, local.at[1])
    save_t.start()
    save_a.wait()
    save_t.wait()


def copies(*refs):
    half = len(refs) // 2
    sems = refs[-1]
    started = []
    for i, (src, dst) in enumerate(zip(refs[:half], refs[half:-1])):
        started.append(pltpu.make_async_copy(src, dst, sems.at[i]))
        started[-1].start()
    for copy in started:
        copy.wait()


def on_device(tokens, cotangent, w_query, w_key, w_value, w_out, gain_query, gain_key, lengths):
    vmem = pl.BlockSpec(memory_space=pltpu.VMEM)
    smem = pl.BlockSpec(memory_space=pltpu.SMEM)
    anywhere = pl.BlockSpec(memory_space=pl.ANY)
    shape = jax.ShapeDtypeStruct
    dma = pltpu.SemaphoreType.DMA
    results = [
        shape((TOK, D), BF),
        shape((TOK, D), BF),
        *[shape((WR, H), F32)] * 4,
        shape((2, H), F32),
    ]
    out = pl.pallas_call(
        kernel,
        name="sublayer",
        out_shape=results,
        in_specs=[smem] + [anywhere] * 2 + [vmem] * 6,
        out_specs=[anywhere] * 2 + [vmem] * 5,
        scratch_shapes=[
            pltpu.VMEM((TOK, D), BF),
            pltpu.VMEM((TOK, D), BF),
            pltpu.VMEM((D, 2 * H), BF),
            pltpu.VMEM((D, 2 * H), BF),
            pltpu.VMEM((TOK, 2 * H), F32),
            pltpu.VMEM((TOK, H), F32),
            pltpu.VMEM((TOK, H), F32),
            pltpu.VMEM((NB * TOK, 2 * H), BF),
            pltpu.VMEM((TOK, H), BF),
            pltpu.VMEM((TOK, H), BF),
            pltpu.VMEM((TOK, H), BF),
            pltpu.VMEM((TOK, 3 * H), BF),
            pltpu.VMEM((NP, 2 * TOK, TOK), F32),
            pltpu.VMEM((NP, 2 * TOK, TOK), F32),
            pltpu.VMEM((H, TOK), F32),
            pltpu.VMEM((H, TOK), F32),
            pltpu.VMEM((NP, 2 * TOK, 2 * H), F32),
            pltpu.VMEM((TOK, 2 * H), F32),
            pltpu.VMEM((2, TOK, D), F32),
            pltpu.VMEM((NP, 2 * WR, 4 * H), F32),
            pltpu.VMEM((WR, 4 * H), F32),
            pltpu.VMEM((TOK, D), BF),
            pltpu.VMEM((TOK, D), BF),
            pltpu.VMEM((9, 8, H), F32),
            pltpu.VMEM((8, 8, H), F32),
            pltpu.VMEM((16, TOK, 2 * H), BF),
            pltpu.VMEM((16, TOK, 2 * H), BF),
            pltpu.VMEM((16, WR, 4 * H), BF),
            pltpu.VMEM((16, WR, 4 * H), BF),
            *[pltpu.VMEM((16, SUB, cols[1]), BF) for cols, _ in ATT + TOKENS for _ in range(2)],
            dma((6 + len(ATT + TOKENS),)),
            *[dma((20,))] * 3,
            dma((8,)),
            dma((2,)),
            *[dma((46 if halves else 30,)) for _, halves in ATT + TOKENS],
        ],
        compiler_params=pltpu.CompilerParams(
            collective_id=0, has_side_effects=True, vmem_limit_bytes=60 * 2**20
        ),
        cost_estimate=pl.CostEstimate(flops=9 * 10**9, bytes_accessed=8 * 2**20, transcendentals=10**6),
    )(
        lengths, tokens, cotangent, w_query, w_key, w_value, w_out,
        gain_query.reshape(1, H), gain_key.reshape(1, H),
    )
    out = pl.pallas_call(
        copies,
        name="results",
        out_shape=results,
        in_specs=[vmem] * 7,
        out_specs=[anywhere] * 7,
        scratch_shapes=[dma((7,))],
    )(*out)
    return tuple(out)


def solution(mesh):
    placed = (
        P("ctx", None),
        P("ctx", None),
        P("ctx", "fsdp"),
        P("ctx", "fsdp"),
        P("ctx", "fsdp"),
        P("ctx", "fsdp"),
        P(),
        P(),
        P(),
    )
    return jax.shard_map(
        on_device,
        mesh=mesh,
        in_specs=placed,
        out_specs=(
            P("ctx", None),
            P("ctx", None),
            P("ctx", "fsdp"),
            P("ctx", "fsdp"),
            P("ctx", "fsdp"),
            P("ctx", "fsdp"),
            P(),
        ),
        check_vma=False,
    )
```

```python
import functools
import math

import jax
import jax.numpy as jnp
from jax import lax
from jax.experimental import pallas as pl
from jax.experimental.pallas import tpu as pltpu
from jax.sharding import PartitionSpec as P

EPS = 1e-06
MESH = pl.DeviceIdType.MESH
BF = jnp.bfloat16
F32 = jnp.float32

TOK = 256
D = 3072
H = 128
WR = 192
NB = 16
NP = 8

OWN, YN, XL, XR, XLY, XRY, OPP, OPPY = range(8)


def nt(a, b):
    return lax.dot_general(a, b, (((1,), (1,)), ((), ())), preferred_element_type=F32)


def tn(a, b):
    return lax.dot_general(a, b, (((0,), (0,)), ((), ())), preferred_element_type=F32)


def nn(a, b):
    return jnp.dot(a, b, preferred_element_type=F32)


class Place:
    def __init__(self):
        c = lax.axis_index("ctx")
        f = lax.axis_index("fsdp")
        self.c, self.f = c, f
        y, x, k = c // 8, (c // 2) % 4, c % 2
        yh, z = f // 8, f % 8
        self.k, self.z, self.y_hi = k, z, yh

        def at(y, x, k, yh, z):
            return ((y * 4 + x) * 2 + k, yh * 8 + z)

        xl, xr, xo = (x + 3) % 4, (x + 1) % 4, (x + 2) % 4
        self.sib = at(y, x, 1 - k, yh, z)
        self.xl = at(y, xl, k, yh, z)
        self.xr = at(y, xr, k, yh, z)
        self.xo = at(y, xo, k, yh, z)
        self.x1 = at(y, x + 1 - 2 * (x % 2), k, yh, z)
        self.yn = at(1 - y, x, k, yh, z)
        self.yh = at(y, x, k, 1 - yh, z)
        self.zl = at(y, x, k, yh, (z + 7) % 8)
        self.zr = at(y, x, k, yh, (z + 1) % 8)
        self.z1 = at(y, x, k, yh, z + 1 - 2 * (z % 2))
        self.z2 = at(y, x, k, yh, (z // 4) * 4 + (z + 2) % 4)
        self.z4 = at(y, x, k, yh, (z + 4) % 8)
        self.all = (
            self.sib, self.xl, self.xr, self.xo, self.yn,
            self.yh, self.zl, self.zr, self.z2, self.z4,
        )
        n = 1 - y
        self.chip = (
            y * 4 + x, n * 4 + x, y * 4 + xl, y * 4 + xr,
            n * 4 + xl, n * 4 + xr, y * 4 + xo, n * 4 + xo,
        )


class Link:
    def __init__(self, send, recv):
        self.send, self.recv, self.sent = send, recv, {}

    def copy(self, m, src, dst, to):
        return pltpu.make_async_remote_copy(
            src_ref=src,
            dst_ref=dst,
            send_sem=self.send,
            recv_sem=self.recv.at[m],
            device_id=to,
            device_id_type=MESH,
        )

    def start(self, m, src, dst, to):
        self.sent[m] = self.copy(m, src, dst, to)
        self.sent[m].start()

    def arrived(self, m):
        self.sent[m].wait_recv()

    def drain(self, sized, to):
        self.copy(0, sized, sized, to).wait_send()


def gather(pc, full, rows, link):
    half = rows // 2
    lo, hi = (0, half), (half, half)
    whole = (0, rows)

    def push(m, t, to, part=whole):
        start = pl.multiple_of(pc.chip[t] * (2 * rows) + pc.k * rows + part[0], 16)
        ref = full.at[pl.ds(start, part[1]), :]
        link.start(m, ref, ref, to)

    def share(t):
        push(11 + t, t, pc.sib)

    push(0, OWN, pc.yn)
    push(1, OWN, pc.xl, hi)
    push(2, OWN, pc.xr, lo)
    push(3, OWN, pc.xl, lo)
    push(4, OWN, pc.xr, hi)
    share(OWN)
    yield ()
    link.arrived(1)
    push(7, XR, pc.xl, hi)
    link.arrived(2)
    push(8, XL, pc.xr, lo)
    yield ()
    link.arrived(0)
    push(5, YN, pc.xl)
    push(6, YN, pc.xr)
    share(YN)
    link.arrived(11 + OWN)
    yield (OWN,)
    link.arrived(3)
    share(XR)
    link.arrived(4)
    share(XL)
    link.arrived(11 + YN)
    yield (YN,)
    link.arrived(8)
    push(9, OPP, pc.yn, lo)
    link.arrived(7)
    push(10, OPP, pc.yn, hi)
    share(OPP)
    link.arrived(11 + XR)
    link.arrived(11 + XL)
    yield (XR, XL)
    link.arrived(5)
    share(XRY)
    link.arrived(6)
    share(XLY)
    link.arrived(11 + OPP)
    yield (OPP,)
    link.arrived(9)
    push(18, OPPY, pc.sib, lo)
    link.arrived(10)
    push(19, OPPY, pc.sib, hi)
    link.arrived(11 + XRY)
    link.arrived(11 + XLY)
    yield (XRY, XLY)
    link.arrived(18)
    link.arrived(19)
    yield (OPPY,)
    link.drain(full.at[pl.ds(0, 15 * rows), :], pc.sib)


def scatter(pc, make, part, own, rows, link, sbuf, rbuf):
    half = rows // 2
    lo, hi, whole = pl.ds(0, half), pl.ds(half, half), pl.ds(0, rows)
    mine = pl.multiple_of(pc.k * rows, rows)
    theirs = pl.multiple_of((1 - pc.k) * rows, rows)

    def made(t):
        make(t)
        sbuf[8 + t] = part[t, pl.ds(theirs, rows), :].astype(BF)
        link.start(11 + t, sbuf.at[8 + t], rbuf.at[8 + t], pc.sib)

    def chip_sum(t):
        link.arrived(11 + t)
        part[t, pl.ds(mine, rows), :] += rbuf[8 + t].astype(F32)

    def add(t, slot, m, rows_of=whole):
        link.arrived(m)
        span = pl.ds(pl.multiple_of(mine + rows_of.start, half), rows_of.size)
        part[t, span, :] += rbuf[slot, rows_of, :].astype(F32)

    def push(m, t, slot, to, rows_of=whole):
        span = pl.ds(pl.multiple_of(mine + rows_of.start, half), rows_of.size)
        sbuf[slot, rows_of, :] = part[t, span, :].astype(BF)
        link.start(m, sbuf.at[slot, rows_of], rbuf.at[slot, rows_of], to)

    made(OPPY)
    made(OPP)
    chip_sum(OPPY)
    push(0, OPPY, 0, pc.yn, lo)
    push(1, OPPY, 0, pc.yn, hi)
    yield
    made(XLY)
    made(XRY)
    chip_sum(XLY)
    push(2, XLY, 1, pc.xl)
    chip_sum(XRY)
    push(3, XRY, 2, pc.xr)
    yield
    made(XL)
    made(XR)
    chip_sum(OPP)
    add(OPP, 0, 0, lo)
    push(4, OPP, 3, pc.xl, lo)
    add(OPP, 0, 1, hi)
    push(5, OPP, 3, pc.xr, hi)
    yield
    chip_sum(XL)
    push(6, XL, 5, pc.xl, hi)
    chip_sum(XR)
    push(7, XR, 6, pc.xr, lo)
    made(YN)
    made(OWN)
    yield
    chip_sum(YN)
    add(XL, 3, 4, lo)
    push(8, XL, 5, pc.xl, lo)
    add(XR, 3, 5, hi)
    push(9, XR, 6, pc.xr, hi)
    yield
    add(YN, 1, 2)
    add(YN, 2, 3)
    push(10, YN, 7, pc.yn)
    yield
    chip_sum(OWN)
    for m in (6, 7, 8, 9, 10):
        link.arrived(m)
    own[...] = part[OWN, pl.ds(mine, rows), :] + (
        rbuf[5].astype(F32) + rbuf[6].astype(F32) + rbuf[7].astype(F32)
    )
    yield
    link.drain(sbuf.at[pl.ds(0, 15)], pc.sib)


SUB = 16
ATT = (((0, 1536), "whole"), ((1536, 1536), "halves"))
TOKENS = (((0, 2048), "whole"), ((2048, 1024), "across"))


ORDER_OF_SUMS = "wgzwzawgzwzwgzywzywgyyzzyyyaawyygzz" + "zyag" * 9


def lane_buffers(cols, mode):
    width = cols[1]
    if mode != "across":
        return [pltpu.VMEM((16, SUB, width), BF)] * 2
    return [pltpu.VMEM((14, SUB, width // 2), BF)] * 2 + [pltpu.VMEM((2, TOK // 2, width // 2), BF)] * 2


RIGHT = ((4, 0), (3, 1), (3, 0), (2, 1), (2, 0), (1, 1), (1, 0))
LEFT = ((4, 1), (3, 0), (3, 1), (2, 0), (2, 1), (1, 0), (1, 1))


def sum_heads(pc, cols, mode, term, out, link, sbuf, rbuf, sin=None, rin=None):
    first, width = cols
    half = width // 2
    full = pl.ds(first, width)
    halves, across = mode == "halves", mode == "across"
    side_rows = TOK // 2
    mine = pl.ds(pl.multiple_of(pc.y_hi * side_rows, side_rows), side_rows)
    theirs = pl.ds(pl.multiple_of((1 - pc.y_hi) * side_rows, side_rows), side_rows)

    def at(chip, u):
        if across:
            start = pl.multiple_of(pc.y_hi * side_rows + chip * SUB, SUB)
            return pl.ds(start, SUB), pl.ds(first + u * half, half)
        return pl.ds(pl.multiple_of(chip * (2 * SUB) + u * SUB, SUB), SUB), full

    def piece(chip, u):
        if not halves:
            return at(chip, u)
        start = pl.multiple_of(chip * (2 * SUB) + pc.y_hi * SUB, SUB)
        return pl.ds(start, SUB), pl.ds(first + u * half, half)

    def owner(distance):
        return (pc.z + 8 + distance) % 8

    if across:
        for u in (0, 1):
            sin[u] = term[theirs, pl.ds(first + u * half, half)].astype(BF)
            link.start(46 + u, sin.at[u], rin.at[u], pc.yh)
        yield
        for u in (0, 1):
            link.arrived(46 + u)
            term[mine, pl.ds(first + u * half, half)] += rin[u].astype(F32)
    right = {m: i for i, m in enumerate(RIGHT)}
    left = {m: 7 + i for i, m in enumerate(LEFT)}
    for i in range(7):
        for side, sign, steps, to in ((right, 1, RIGHT, pc.zr), (left, -1, LEFT, pc.zl)):
            d, u = steps[i]
            value = term[at(owner(sign * d), u)]
            before = side.get((d + 1, u))
            if before is not None:
                link.arrived(before)
                value = value + rbuf[before].astype(F32)
            m = side[(d, u)]
            sbuf[m] = value.astype(BF)
            link.start(m, sbuf.at[m], rbuf.at[m], to)
        yield

    def total(u):
        value = term[at(pc.z, u)]
        for m in (right[(1, u)], left[(1, u)]):
            link.arrived(m)
            value = value + rbuf[m].astype(F32)
        return value.astype(BF)

    def forward(m, chip, u, to):
        ref = out.at[piece(chip, u)]
        link.start(m, ref, ref, to)

    def spread(u):
        forward(16 + u, pc.z, u, pc.zr)
        forward(23 + u, pc.z, u, pc.zl)
        if halves or across:
            forward(30 + u, pc.z, u, pc.yh)

    for u in (0, 1):
        if across:
            out[at(pc.z, u)] = total(u)
            spread(u)
            yield
            continue
        sbuf[14 + u] = total(u)
        if not halves:
            link.start(14 + u, sbuf.at[14 + u], rbuf.at[14 + u], pc.yh)
        elif u == 1:
            link.start(14, sbuf.at[14 + 1 - pc.y_hi], rbuf.at[14], pc.yh)
        yield
    for u in () if across else (0, 1):
        if not halves:
            link.arrived(14 + u)
            both = sbuf[14 + u].astype(F32) + rbuf[14 + u].astype(F32)
            out[at(pc.z, u)] = both.astype(BF)
        elif u == 0:
            link.arrived(14)
            both = sbuf[14 + pc.y_hi].astype(F32) + rbuf[14].astype(F32)
            out[at(pc.z, pc.y_hi)] = both.astype(BF)
        spread(u)
        yield

    def hop_id(base, hop, u):
        return base + (2 * (hop - 1) + u if hop < 4 else 6)

    extra = 32
    for hop in (1, 2, 3, 4):
        for u in (0, 1):
            for base, sign, to, last in ((16, -1, pc.zr, 0), (23, 1, pc.zl, 1)):
                if hop == 4 and u != last:
                    continue
                link.arrived(hop_id(base, hop, u))
                if hop < 3 or (hop == 3 and u == last):
                    forward(hop_id(base, hop + 1, u), owner(sign * hop), u, to)
                if halves or across:
                    forward(extra, owner(sign * hop), u, pc.yh)
                    extra += 1
            yield
    if halves or across:
        for m in range(30, extra):
            link.arrived(m)
    link.drain(term.at[pl.ds(0, 15 * SUB), full], pc.zr)


def sum_small(pc, value_ref, link, rbuf):
    for m, to in enumerate((pc.sib, pc.x1, pc.xo, pc.yn, pc.z1, pc.z2, pc.z4, pc.yh)):
        link.start(m, value_ref.at[m], rbuf.at[m], to)
        yield "sent"
        link.arrived(m)
        value_ref[m + 1] = value_ref[m] + rbuf[m]
    link.drain(value_ref.at[pl.ds(0, 8)], pc.sib)


def inv_rms(values):
    return lax.rsqrt(jnp.mean(values * values, -1, keepdims=True) + EPS)


def norm_back(grad, unit, rms, gain):
    scaled = grad * gain
    return rms * (scaled - unit * jnp.mean(scaled * unit, -1, keepdims=True))


def kernel(
    length_ref, tokens_in, cotangent_in, w_query, w_key, w_value, w_out, gain_query, gain_key,
    attended, grad_tokens, g_query, g_key, g_value, g_out, g_gains,
    tokens, cotangent, wkv, wqo, kvp, qp, gacc, kvfull, qn, gb, mixed, dc, probs, gprobs, oacc, qacc,
    dkv, dkv_own, term, wpart, w_own, att_v, tok_v,
    gain_v, gain_r, s_dkv, r_dkv, s_w, r_w, *rest,
):
    lanes, rest = [], list(rest)
    for cols, mode in ATT + TOKENS:
        n = len(lane_buffers(cols, mode))
        lanes.append(rest[:n])
        del rest[:n]
    sent, r_kv, r_qo, r_keys, r_gain, local, *r_lanes = rest
    pc = Place()
    inv_root = 1.0 / math.sqrt(H)
    length = length_ref[0]

    barrier = pltpu.get_barrier_semaphore()
    for other in pc.all:
        pl.semaphore_signal(barrier, inc=1, device_id=other, device_id_type=MESH)
    load_t = pltpu.make_async_copy(tokens_in, tokens, local.at[0])
    load_t.start()
    load_c = pltpu.make_async_copy(cotangent_in, cotangent, local.at[1])
    load_c.start()

    own_rows = pl.ds(pl.multiple_of(pc.c * WR, WR), WR)
    for full, left, right in ((wkv, w_key, w_value), (wqo, w_query, w_out)):
        full[own_rows, 0:H] = left[...]
        full[own_rows, H : 2 * H] = right[...]
    for total in (kvp, qp, gacc, oacc, qacc, gain_v):
        total[...] = jnp.zeros_like(total)
    pl.semaphore_wait(barrier, len(pc.all))

    def model_rows(t):
        return pl.ds(pl.multiple_of(pc.chip[t] * (2 * WR), 2 * WR), 2 * WR)

    def key_rows(t):
        return pl.ds(pl.multiple_of(pc.chip[t] * (2 * TOK), 2 * TOK), 2 * TOK)

    def unit_of(values):
        rms = inv_rms(values)
        return values * rms, rms

    def step(work, n=1):
        for _ in range(n):
            next(work, None)

    def each(works):
        for work in works:
            step(work)

    def project_kv(chips):
        for t in chips:
            r = model_rows(t)
            kvp[...] += nn(tokens[:, r], wkv[r, :])

    def project_qo(chips):
        for t in chips:
            r = model_rows(t)
            qp[...] += nn(tokens[:, r], wqo[r, 0:H])
            gacc[...] += nn(cotangent[:, r], wqo[r, H : 2 * H])

    def run(work, use, n):
        for _ in range(n):
            use(next(work, ()))

    gain_q, gain_k = gain_query[...], gain_key[...]
    first = gather(pc, wkv, WR, Link(sent.at[0], r_kv))
    second = gather(pc, wqo, WR, Link(sent.at[1], r_qo))
    step(first, 2)
    load_t.wait()
    load_c.wait()
    run(first, project_kv, 3)
    step(second)
    run(first, project_kv, 1)
    step(second)
    run(second, project_qo, 1)
    run(first, project_kv, 2)
    run(second, project_qo, 1)
    own_keys = pl.ds(pl.multiple_of(pc.c * TOK, TOK), TOK)
    kvfull[own_keys, 0:H] = (unit_of(kvp[:, 0:H])[0] * gain_k).astype(BF)
    kvfull[own_keys, H : 2 * H] = kvp[:, H : 2 * H].astype(BF)
    third = gather(pc, kvfull, TOK, Link(sent.at[2], r_keys))
    step(third)
    run(second, project_qo, 2)
    step(third)
    run(second, project_qo, 2)
    step(first)
    step(second)
    qn[...] = (unit_of(qp[...])[0] * gain_q).astype(BF)
    gb[...] = gacc[...].astype(BF)

    denom = jnp.zeros((1, TOK), F32)
    for chips in third:
        for t in chips:
            keys, values = kvfull[key_rows(t), 0:H], kvfull[key_rows(t), H : 2 * H]
            scores = nt(keys, qn[...]) * inv_root
            place = pc.chip[t] * (2 * TOK) + lax.broadcasted_iota(jnp.int32, scores.shape, 0)
            weights = jnp.where(place < length, jnp.exp(scores), 0.0)
            probs[t] = weights
            denom = denom + jnp.sum(weights, 0, keepdims=True)
            oacc[...] += tn(values, weights.astype(BF))
            gprobs[t] = nt(values, gb[...])

    inv_denom = 1.0 / denom
    mixed_t = oacc[...] / denom
    mixed[...] = mixed_t.T.astype(BF)
    delta = jnp.sum(gb[...].astype(F32).T * mixed_t.astype(BF).astype(F32), 0, keepdims=True)

    term[0] = nt(mixed[...], wqo[:, H : 2 * H])
    def sums(config, start, src, dst):
        return [
            sum_heads(pc, *config[i], src, dst, Link(sent.at[6 + n], r_lanes[n]), *lanes[n])
            for i, n in enumerate(range(start, start + len(config)))
        ]

    att = sums(ATT, 0, term.at[0], att_v)
    each(att)

    def keys_back(t):
        keys = kvfull[key_rows(t), 0:H]
        probs_t = probs[t] * inv_denom
        scores_b = (probs_t * (gprobs[t] - delta)).astype(BF)
        qacc[...] += tn(keys, scores_b)
        dkv[t, :, 0:H] = nn(scores_b, qn[...]) * inv_root
        dkv[t, :, H : 2 * H] = nn(probs_t.astype(BF), gb[...])

    for _ in scatter(pc, keys_back, dkv, dkv_own, TOK, Link(sent.at[3], r_kv), s_dkv, r_dkv):
        each(att)

    grad_qn = qacc[...].T * inv_root
    grad_kn = dkv_own[:, 0:H]
    unit_q, rms_q = unit_of(qp[...])
    unit_k, rms_k = unit_of(kvp[:, 0:H])
    dc[:, 0:H] = norm_back(grad_qn, unit_q, rms_q, gain_q).astype(BF)
    dc[:, H : 2 * H] = norm_back(grad_kn, unit_k, rms_k, gain_k).astype(BF)
    dc[:, 2 * H : 3 * H] = dkv_own[:, H : 2 * H].astype(BF)

    term[1] = nt(dc[:, 0:H], wqo[:, 0:H]) + nt(dc[:, H : 3 * H], wkv[...])
    tok = sums(TOKENS, len(ATT), term.at[1], tok_v)
    for work in tok[::-1]:
        step(work)

    gain_v[0, 0:1, :] = jnp.sum(grad_qn * unit_q, 0, keepdims=True)
    gain_v[0, 1:2, :] = jnp.sum(grad_kn * unit_k, 0, keepdims=True)
    gains = sum_small(pc, gain_v, Link(sent.at[5], r_gain), gain_r)

    def weights_back(t):
        r = model_rows(t)
        wpart[t, :, 0 : 3 * H] = tn(tokens[:, r], dc[...])
        wpart[t, :, 3 * H : 4 * H] = tn(cotangent[:, r], mixed[...])

    grads = scatter(pc, weights_back, wpart, w_own, WR, Link(sent.at[4], r_qo), s_w, r_w)
    works = {"w": [grads], "g": [gains], "a": att, "z": tok[:1], "y": tok[1:]}
    for name in ORDER_OF_SUMS:
        each(works[name])
    save_a = pltpu.make_async_copy(att_v, attended, local.at[0])
    save_a.start()
    for i, g in enumerate((g_query, g_key, g_value, g_out)):
        g[...] = w_own[:, i * H : (i + 1) * H]
    g_gains[...] = gain_v[8, 0:2, :]
    save_t = pltpu.make_async_copy(tok_v, grad_tokens, local.at[1])
    save_t.start()
    save_a.wait()
    save_t.wait()


def copies(*refs):
    half = len(refs) // 2
    sems = refs[-1]
    started = []
    for i, (src, dst) in enumerate(zip(refs[:half], refs[half:-1])):
        started.append(pltpu.make_async_copy(src, dst, sems.at[i]))
        started[-1].start()
    for copy in started:
        copy.wait()


def on_device(tokens, cotangent, w_query, w_key, w_value, w_out, gain_query, gain_key, lengths):
    vmem = pl.BlockSpec(memory_space=pltpu.VMEM)
    smem = pl.BlockSpec(memory_space=pltpu.SMEM)
    anywhere = pl.BlockSpec(memory_space=pl.ANY)
    shape = jax.ShapeDtypeStruct
    dma = pltpu.SemaphoreType.DMA
    results = [
        shape((TOK, D), BF),
        shape((TOK, D), BF),
        *[shape((WR, H), F32)] * 4,
        shape((2, H), F32),
    ]
    out = pl.pallas_call(
        kernel,
        name="sublayer",
        out_shape=results,
        in_specs=[smem] + [anywhere] * 2 + [vmem] * 6,
        out_specs=[anywhere] * 2 + [vmem] * 5,
        scratch_shapes=[
            pltpu.VMEM((TOK, D), BF),
            pltpu.VMEM((TOK, D), BF),
            pltpu.VMEM((D, 2 * H), BF),
            pltpu.VMEM((D, 2 * H), BF),
            pltpu.VMEM((TOK, 2 * H), F32),
            pltpu.VMEM((TOK, H), F32),
            pltpu.VMEM((TOK, H), F32),
            pltpu.VMEM((NB * TOK, 2 * H), BF),
            pltpu.VMEM((TOK, H), BF),
            pltpu.VMEM((TOK, H), BF),
            pltpu.VMEM((TOK, H), BF),
            pltpu.VMEM((TOK, 3 * H), BF),
            pltpu.VMEM((NP, 2 * TOK, TOK), F32),
            pltpu.VMEM((NP, 2 * TOK, TOK), F32),
            pltpu.VMEM((H, TOK), F32),
            pltpu.VMEM((H, TOK), F32),
            pltpu.VMEM((NP, 2 * TOK, 2 * H), F32),
            pltpu.VMEM((TOK, 2 * H), F32),
            pltpu.VMEM((2, TOK, D), F32),
            pltpu.VMEM((NP, 2 * WR, 4 * H), F32),
            pltpu.VMEM((WR, 4 * H), F32),
            pltpu.VMEM((TOK, D), BF),
            pltpu.VMEM((TOK, D), BF),
            pltpu.VMEM((9, 8, H), F32),
            pltpu.VMEM((8, 8, H), F32),
            pltpu.VMEM((16, TOK, 2 * H), BF),
            pltpu.VMEM((16, TOK, 2 * H), BF),
            pltpu.VMEM((16, WR, 4 * H), BF),
            pltpu.VMEM((16, WR, 4 * H), BF),
            *[b for cols, mode in ATT + TOKENS for b in lane_buffers(cols, mode)],
            dma((6 + len(ATT + TOKENS),)),
            *[dma((20,))] * 3,
            dma((8,)),
            dma((2,)),
            *[dma((30 if mode == "whole" else 48,)) for _, mode in ATT + TOKENS],
        ],
        compiler_params=pltpu.CompilerParams(
            collective_id=0, has_side_effects=True, vmem_limit_bytes=60 * 2**20
        ),
        cost_estimate=pl.CostEstimate(flops=9 * 10**9, bytes_accessed=8 * 2**20, transcendentals=10**6),
    )(
        lengths, tokens, cotangent, w_query, w_key, w_value, w_out,
        gain_query.reshape(1, H), gain_key.reshape(1, H),
    )
    out = pl.pallas_call(
        copies,
        name="results",
        out_shape=results,
        in_specs=[vmem] * 7,
        out_specs=[anywhere] * 7,
        scratch_shapes=[dma((7,))],
    )(*out)
    return tuple(out)


def solution(mesh):
    placed = (
        P("ctx", None),
        P("ctx", None),
        P("ctx", "fsdp"),
        P("ctx", "fsdp"),
        P("ctx", "fsdp"),
        P("ctx", "fsdp"),
        P(),
        P(),
        P(),
    )
    return jax.shard_map(
        on_device,
        mesh=mesh,
        in_specs=placed,
        out_specs=(
            P("ctx", None),
            P("ctx", None),
            P("ctx", "fsdp"),
            P("ctx", "fsdp"),
            P("ctx", "fsdp"),
            P("ctx", "fsdp"),
            P(),
        ),
        check_vma=False,
    )
```

```python
import math

import jax
import jax.numpy as jnp
from jax import lax
from jax.experimental import pallas as pl
from jax.experimental.pallas import tpu as pltpu
from jax.sharding import PartitionSpec as P

EPS = 1e-06
MESH = pl.DeviceIdType.MESH
BF = jnp.bfloat16
F32 = jnp.float32

TOK = 256
D = 3072
H = 128
WR = 192
NB = 16
NP = 8

OWN, YN, XL, XR, XLY, XRY, OPP, OPPY = range(8)


def nt(a, b):
    return lax.dot_general(a, b, (((1,), (1,)), ((), ())), preferred_element_type=F32)


def tn(a, b):
    return lax.dot_general(a, b, (((0,), (0,)), ((), ())), preferred_element_type=F32)


def nn(a, b):
    return jnp.dot(a, b, preferred_element_type=F32)


class Place:
    def __init__(self):
        c = lax.axis_index("ctx")
        f = lax.axis_index("fsdp")
        self.c, self.f = c, f
        y, x, k = c // 8, (c // 2) % 4, c % 2
        yh, z = f // 8, f % 8
        self.k, self.z, self.y_hi = k, z, yh

        def at(y, x, k, yh, z):
            return ((y * 4 + x) * 2 + k, yh * 8 + z)

        xl, xr, xo = (x + 3) % 4, (x + 1) % 4, (x + 2) % 4
        self.sib = at(y, x, 1 - k, yh, z)
        self.xl = at(y, xl, k, yh, z)
        self.xr = at(y, xr, k, yh, z)
        self.xo = at(y, xo, k, yh, z)
        self.x1 = at(y, x + 1 - 2 * (x % 2), k, yh, z)
        self.yn = at(1 - y, x, k, yh, z)
        self.yh = at(y, x, k, 1 - yh, z)
        self.zl = at(y, x, k, yh, (z + 7) % 8)
        self.zr = at(y, x, k, yh, (z + 1) % 8)
        self.z1 = at(y, x, k, yh, z + 1 - 2 * (z % 2))
        self.z2 = at(y, x, k, yh, (z // 4) * 4 + (z + 2) % 4)
        self.z4 = at(y, x, k, yh, (z + 4) % 8)
        self.all = (
            self.sib, self.xl, self.xr, self.xo, self.yn,
            self.yh, self.zl, self.zr, self.z2, self.z4,
        )
        n = 1 - y
        self.chip = (
            y * 4 + x, n * 4 + x, y * 4 + xl, y * 4 + xr,
            n * 4 + xl, n * 4 + xr, y * 4 + xo, n * 4 + xo,
        )


class Link:
    def __init__(self, send, recv):
        self.send, self.recv, self.sent = send, recv, {}

    def copy(self, m, src, dst, to):
        return pltpu.make_async_remote_copy(
            src_ref=src,
            dst_ref=dst,
            send_sem=self.send,
            recv_sem=self.recv.at[m],
            device_id=to,
            device_id_type=MESH,
        )

    def start(self, m, src, dst, to):
        self.sent[m] = self.copy(m, src, dst, to)
        self.sent[m].start()

    def arrived(self, m):
        self.sent[m].wait_recv()

    def drain(self, sized, to):
        self.copy(0, sized, sized, to).wait_send()


def gather(pc, full, rows, link):
    half = rows // 2
    lo, hi = (0, half), (half, half)
    whole = (0, rows)

    def push(m, t, to, part=whole):
        start = pl.multiple_of(pc.chip[t] * (2 * rows) + pc.k * rows + part[0], 16)
        ref = full.at[pl.ds(start, part[1]), :]
        link.start(m, ref, ref, to)

    def share(t):
        push(11 + t, t, pc.sib)

    push(0, OWN, pc.yn)
    push(1, OWN, pc.xl, hi)
    push(2, OWN, pc.xr, lo)
    push(3, OWN, pc.xl, lo)
    push(4, OWN, pc.xr, hi)
    share(OWN)
    yield ()
    link.arrived(1)
    push(7, XR, pc.xl, hi)
    link.arrived(2)
    push(8, XL, pc.xr, lo)
    yield ()
    link.arrived(0)
    push(5, YN, pc.xl)
    push(6, YN, pc.xr)
    share(YN)
    link.arrived(11 + OWN)
    yield (OWN,)
    link.arrived(3)
    share(XR)
    link.arrived(4)
    share(XL)
    link.arrived(11 + YN)
    yield (YN,)
    link.arrived(8)
    push(9, OPP, pc.yn, lo)
    link.arrived(7)
    push(10, OPP, pc.yn, hi)
    share(OPP)
    link.arrived(11 + XR)
    link.arrived(11 + XL)
    yield (XR, XL)
    link.arrived(5)
    share(XRY)
    link.arrived(6)
    share(XLY)
    link.arrived(11 + OPP)
    yield (OPP,)
    link.arrived(9)
    push(18, OPPY, pc.sib, lo)
    link.arrived(10)
    push(19, OPPY, pc.sib, hi)
    link.arrived(11 + XRY)
    link.arrived(11 + XLY)
    yield (XRY, XLY)
    link.arrived(18)
    link.arrived(19)
    yield (OPPY,)
    link.drain(full.at[pl.ds(0, 15 * rows), :], pc.sib)


def scatter(pc, make, part, own, rows, link, sbuf, rbuf):
    half = rows // 2
    lo, hi, whole = pl.ds(0, half), pl.ds(half, half), pl.ds(0, rows)
    mine = pl.multiple_of(pc.k * rows, rows)
    theirs = pl.multiple_of((1 - pc.k) * rows, rows)

    def made(t):
        make(t)
        sbuf[8 + t] = part[t, pl.ds(theirs, rows), :].astype(BF)
        link.start(11 + t, sbuf.at[8 + t], rbuf.at[8 + t], pc.sib)

    def chip_sum(t):
        link.arrived(11 + t)
        part[t, pl.ds(mine, rows), :] += rbuf[8 + t].astype(F32)

    def add(t, slot, m, rows_of=whole):
        link.arrived(m)
        span = pl.ds(pl.multiple_of(mine + rows_of.start, half), rows_of.size)
        part[t, span, :] += rbuf[slot, rows_of, :].astype(F32)

    def push(m, t, slot, to, rows_of=whole):
        span = pl.ds(pl.multiple_of(mine + rows_of.start, half), rows_of.size)
        sbuf[slot, rows_of, :] = part[t, span, :].astype(BF)
        link.start(m, sbuf.at[slot, rows_of], rbuf.at[slot, rows_of], to)

    made(OPPY)
    made(OPP)
    yield
    chip_sum(OPPY)
    push(0, OPPY, 0, pc.yn, lo)
    push(1, OPPY, 0, pc.yn, hi)
    made(XLY)
    made(XRY)
    yield
    chip_sum(XLY)
    push(2, XLY, 1, pc.xl)
    chip_sum(XRY)
    push(3, XRY, 2, pc.xr)
    made(YN)
    made(XL)
    yield
    made(XR)
    chip_sum(OPP)
    add(OPP, 0, 0, lo)
    push(4, OPP, 3, pc.xl, lo)
    add(OPP, 0, 1, hi)
    push(5, OPP, 3, pc.xr, hi)
    yield
    chip_sum(YN)
    add(YN, 1, 2)
    add(YN, 2, 3)
    push(10, YN, 7, pc.yn)
    yield
    chip_sum(XL)
    push(6, XL, 5, pc.xl, hi)
    chip_sum(XR)
    push(7, XR, 6, pc.xr, lo)
    made(OWN)
    yield
    add(XL, 3, 4, lo)
    push(8, XL, 5, pc.xl, lo)
    add(XR, 3, 5, hi)
    push(9, XR, 6, pc.xr, hi)
    yield
    chip_sum(OWN)
    for m in (6, 7, 8, 9, 10):
        link.arrived(m)
    own[...] = part[OWN, pl.ds(mine, rows), :] + (
        rbuf[5].astype(F32) + rbuf[6].astype(F32) + rbuf[7].astype(F32)
    )
    yield
    link.drain(sbuf.at[pl.ds(0, 15)], pc.sib)


SUB = 16
ATT = (((0, D), "halves"),)
TOKENS = (((0, 1536), "whole"), ((1536, 1536), "whole"))


ORDER_OF_SUMS = 'wzwzawzawzwzzwzzaagwzz' + "azgw" * 14


def lane_buffers(cols, mode):
    width = cols[1]
    if mode != "across":
        return [pltpu.VMEM((16, SUB, width), BF)] * 2
    return [pltpu.VMEM((14, SUB, width // 2), BF)] * 2 + [pltpu.VMEM((2, TOK // 2, width // 2), BF)] * 2


RIGHT = ((4, 0), (3, 1), (3, 0), (2, 1), (2, 0), (1, 1), (1, 0))
LEFT = ((4, 1), (3, 0), (3, 1), (2, 0), (2, 1), (1, 0), (1, 1))


def sum_heads(pc, cols, mode, term, out, link, sbuf, rbuf, sin=None, rin=None):
    first, width = cols
    half = width // 2
    full = pl.ds(first, width)
    halves, across = mode == "halves", mode == "across"
    side_rows = TOK // 2
    mine = pl.ds(pl.multiple_of(pc.y_hi * side_rows, side_rows), side_rows)
    theirs = pl.ds(pl.multiple_of((1 - pc.y_hi) * side_rows, side_rows), side_rows)

    def at(chip, u):
        if across:
            start = pl.multiple_of(pc.y_hi * side_rows + chip * SUB, SUB)
            return pl.ds(start, SUB), pl.ds(first + u * half, half)
        return pl.ds(pl.multiple_of(chip * (2 * SUB) + u * SUB, SUB), SUB), full

    def piece(chip, u):
        if not halves:
            return at(chip, u)
        start = pl.multiple_of(chip * (2 * SUB) + pc.y_hi * SUB, SUB)
        return pl.ds(start, SUB), pl.ds(first + u * half, half)

    def owner(distance):
        return (pc.z + 8 + distance) % 8

    if across:
        for u in (0, 1):
            sin[u] = term[theirs, pl.ds(first + u * half, half)].astype(BF)
            link.start(46 + u, sin.at[u], rin.at[u], pc.yh)
        yield
        for u in (0, 1):
            link.arrived(46 + u)
            term[mine, pl.ds(first + u * half, half)] += rin[u].astype(F32)
    right = {m: i for i, m in enumerate(RIGHT)}
    left = {m: 7 + i for i, m in enumerate(LEFT)}
    for i in range(7):
        for side, sign, steps, to in ((right, 1, RIGHT, pc.zr), (left, -1, LEFT, pc.zl)):
            d, u = steps[i]
            value = term[at(owner(sign * d), u)]
            before = side.get((d + 1, u))
            if before is not None:
                link.arrived(before)
                value = value + rbuf[before].astype(F32)
            m = side[(d, u)]
            sbuf[m] = value.astype(BF)
            link.start(m, sbuf.at[m], rbuf.at[m], to)
        yield

    def total(u):
        value = term[at(pc.z, u)]
        for m in (right[(1, u)], left[(1, u)]):
            link.arrived(m)
            value = value + rbuf[m].astype(F32)
        return value.astype(BF)

    def forward(m, chip, u, to):
        ref = out.at[piece(chip, u)]
        link.start(m, ref, ref, to)

    def spread(u):
        forward(16 + u, pc.z, u, pc.zr)
        forward(23 + u, pc.z, u, pc.zl)
        if halves or across:
            forward(30 + u, pc.z, u, pc.yh)

    for u in (0, 1):
        if across:
            out[at(pc.z, u)] = total(u)
            spread(u)
            yield
            continue
        sbuf[14 + u] = total(u)
        if not halves:
            link.start(14 + u, sbuf.at[14 + u], rbuf.at[14 + u], pc.yh)
        elif u == 1:
            link.start(14, sbuf.at[14 + 1 - pc.y_hi], rbuf.at[14], pc.yh)
        yield
    for u in () if across else (0, 1):
        if not halves:
            link.arrived(14 + u)
            both = sbuf[14 + u].astype(F32) + rbuf[14 + u].astype(F32)
            out[at(pc.z, u)] = both.astype(BF)
        elif u == 0:
            link.arrived(14)
            both = sbuf[14 + pc.y_hi].astype(F32) + rbuf[14].astype(F32)
            out[at(pc.z, pc.y_hi)] = both.astype(BF)
        spread(u)
        yield

    def hop_id(base, hop, u):
        return base + (2 * (hop - 1) + u if hop < 4 else 6)

    extra = 32
    for hop in (1, 2, 3, 4):
        for u in (0, 1):
            for base, sign, to, last in ((16, -1, pc.zr, 0), (23, 1, pc.zl, 1)):
                if hop == 4 and u != last:
                    continue
                link.arrived(hop_id(base, hop, u))
                if hop < 3 or (hop == 3 and u == last):
                    forward(hop_id(base, hop + 1, u), owner(sign * hop), u, to)
                if halves or across:
                    forward(extra, owner(sign * hop), u, pc.yh)
                    extra += 1
            yield
    if halves or across:
        for m in range(30, extra):
            link.arrived(m)
    link.drain(term.at[pl.ds(0, 15 * SUB), full], pc.zr)


def sum_small(pc, value_ref, link, rbuf):
    for m, to in enumerate((pc.sib, pc.x1, pc.xo, pc.yn, pc.z1, pc.z2, pc.z4, pc.yh)):
        link.start(m, value_ref.at[m], rbuf.at[m], to)
        yield "sent"
        link.arrived(m)
        value_ref[m + 1] = value_ref[m] + rbuf[m]
    link.drain(value_ref.at[pl.ds(0, 8)], pc.sib)


def inv_rms(values):
    return lax.rsqrt(jnp.mean(values * values, -1, keepdims=True) + EPS)


def norm_back(grad, unit, rms, gain):
    scaled = grad * gain
    return rms * (scaled - unit * jnp.mean(scaled * unit, -1, keepdims=True))


def kernel(
    length_ref, tokens_in, cotangent_in, w_query, w_key, w_value, w_out, gain_query, gain_key,
    attended, grad_tokens, g_query, g_key, g_value, g_out, g_gains,
    tokens, cotangent, wkv, wqo, kvp, qp, gacc, kvfull, qn, gb, mixed, dc, probs, gprobs, oacc, qacc,
    dkv, dkv_own, term, wpart, w_own, att_v, tok_v,
    gain_v, gain_r, s_dkv, r_dkv, s_w, r_w, *rest,
):
    lanes, rest = [], list(rest)
    for cols, mode in ATT + TOKENS:
        n = len(lane_buffers(cols, mode))
        lanes.append(rest[:n])
        del rest[:n]
    sent, r_kv, r_qo, r_keys, r_gain, local, *r_lanes = rest
    pc = Place()
    inv_root = 1.0 / math.sqrt(H)
    length = length_ref[0]

    barrier = pltpu.get_barrier_semaphore()
    for other in pc.all:
        pl.semaphore_signal(barrier, inc=1, device_id=other, device_id_type=MESH)
    load_t = pltpu.make_async_copy(tokens_in, tokens, local.at[0])
    load_t.start()
    load_c = pltpu.make_async_copy(cotangent_in, cotangent, local.at[1])
    load_c.start()

    own_rows = pl.ds(pl.multiple_of(pc.c * WR, WR), WR)
    for full, left, right in ((wkv, w_key, w_value), (wqo, w_query, w_out)):
        full[own_rows, 0:H] = left[...]
        full[own_rows, H : 2 * H] = right[...]
    for total in (kvp, qp, gacc, oacc, qacc, gain_v):
        total[...] = jnp.zeros_like(total)
    pl.semaphore_wait(barrier, len(pc.all))

    def model_rows(t):
        return pl.ds(pl.multiple_of(pc.chip[t] * (2 * WR), 2 * WR), 2 * WR)

    def key_rows(t):
        return pl.ds(pl.multiple_of(pc.chip[t] * (2 * TOK), 2 * TOK), 2 * TOK)

    def unit_of(values):
        rms = inv_rms(values)
        return values * rms, rms

    def step(work, n=1):
        for _ in range(n):
            next(work, None)

    def each(works):
        for work in works:
            step(work)

    def project_kv(chips):
        for t in chips:
            r = model_rows(t)
            kvp[...] += nn(tokens[:, r], wkv[r, :])

    def project_qo(chips):
        for t in chips:
            r = model_rows(t)
            qp[...] += nn(tokens[:, r], wqo[r, 0:H])
            gacc[...] += nn(cotangent[:, r], wqo[r, H : 2 * H])

    def run(work, use, n):
        for _ in range(n):
            use(next(work, ()))

    gain_q, gain_k = gain_query[...], gain_key[...]
    first = gather(pc, wkv, WR, Link(sent.at[0], r_kv))
    second = gather(pc, wqo, WR, Link(sent.at[1], r_qo))
    step(first, 2)
    load_t.wait()
    load_c.wait()
    run(first, project_kv, 3)
    step(second)
    run(first, project_kv, 1)
    step(second)
    run(second, project_qo, 1)
    run(first, project_kv, 2)
    run(second, project_qo, 1)
    own_keys = pl.ds(pl.multiple_of(pc.c * TOK, TOK), TOK)
    kvfull[own_keys, 0:H] = (unit_of(kvp[:, 0:H])[0] * gain_k).astype(BF)
    kvfull[own_keys, H : 2 * H] = kvp[:, H : 2 * H].astype(BF)
    third = gather(pc, kvfull, TOK, Link(sent.at[2], r_keys))
    step(third)
    run(second, project_qo, 2)
    step(third)
    run(second, project_qo, 2)
    step(first)
    step(second)
    qn[...] = (unit_of(qp[...])[0] * gain_q).astype(BF)
    gb[...] = gacc[...].astype(BF)

    denom = jnp.zeros((1, TOK), F32)
    for chips in third:
        for t in chips:
            keys, values = kvfull[key_rows(t), 0:H], kvfull[key_rows(t), H : 2 * H]
            scores = nt(keys, qn[...]) * inv_root
            place = pc.chip[t] * (2 * TOK) + lax.broadcasted_iota(jnp.int32, scores.shape, 0)
            weights = jnp.where(place < length, jnp.exp(scores), 0.0)
            probs[t] = weights
            denom = denom + jnp.sum(weights, 0, keepdims=True)
            oacc[...] += tn(values, weights.astype(BF))
            gprobs[t] = nt(values, gb[...])

    inv_denom = 1.0 / denom
    mixed_t = oacc[...] / denom
    mixed[...] = mixed_t.T.astype(BF)
    delta = jnp.sum(gb[...].astype(F32).T * mixed_t.astype(BF).astype(F32), 0, keepdims=True)

    term[0] = nt(mixed[...], wqo[:, H : 2 * H])
    def sums(config, start, src, dst):
        return [
            sum_heads(pc, *config[i], src, dst, Link(sent.at[6 + n], r_lanes[n]), *lanes[n])
            for i, n in enumerate(range(start, start + len(config)))
        ]

    att = sums(ATT, 0, term.at[0], att_v)
    each(att)

    def keys_back(t):
        keys = kvfull[key_rows(t), 0:H]
        probs_t = probs[t] * inv_denom
        scores_b = (probs_t * (gprobs[t] - delta)).astype(BF)
        qacc[...] += tn(keys, scores_b)
        dkv[t, :, 0:H] = nn(scores_b, qn[...]) * inv_root
        dkv[t, :, H : 2 * H] = nn(probs_t.astype(BF), gb[...])

    for i, _ in enumerate(scatter(pc, keys_back, dkv, dkv_own, TOK, Link(sent.at[3], r_kv), s_dkv, r_dkv)):
        if 0 < i < 7:
            each(att)

    grad_qn = qacc[...].T * inv_root
    grad_kn = dkv_own[:, 0:H]
    unit_q, rms_q = unit_of(qp[...])
    unit_k, rms_k = unit_of(kvp[:, 0:H])
    dc[:, 0:H] = norm_back(grad_qn, unit_q, rms_q, gain_q).astype(BF)
    dc[:, H : 2 * H] = norm_back(grad_kn, unit_k, rms_k, gain_k).astype(BF)
    dc[:, 2 * H : 3 * H] = dkv_own[:, H : 2 * H].astype(BF)

    term[1] = nt(dc[:, 0:H], wqo[:, 0:H]) + nt(dc[:, H : 3 * H], wkv[...])
    tok = sums(TOKENS, len(ATT), term.at[1], tok_v)
    step(tok[0])

    gain_v[0, 0:1, :] = jnp.sum(grad_qn * unit_q, 0, keepdims=True)
    gain_v[0, 1:2, :] = jnp.sum(grad_kn * unit_k, 0, keepdims=True)
    gains = sum_small(pc, gain_v, Link(sent.at[5], r_gain), gain_r)

    def weights_back(t):
        r = model_rows(t)
        wpart[t, :, 0 : 3 * H] = tn(tokens[:, r], dc[...])
        wpart[t, :, 3 * H : 4 * H] = tn(cotangent[:, r], mixed[...])

    grads = scatter(pc, weights_back, wpart, w_own, WR, Link(sent.at[4], r_qo), s_w, r_w)
    works = {"w": [grads], "g": [gains], "a": att, "z": tok}
    for name in ORDER_OF_SUMS:
        each(works[name])
    save_a = pltpu.make_async_copy(att_v, attended, local.at[0])
    save_a.start()
    for i, g in enumerate((g_query, g_key, g_value, g_out)):
        g[...] = w_own[:, i * H : (i + 1) * H]
    g_gains[...] = gain_v[8, 0:2, :]
    save_t = pltpu.make_async_copy(tok_v, grad_tokens, local.at[1])
    save_t.start()
    save_a.wait()
    save_t.wait()


def copies(*refs):
    half = len(refs) // 2
    sems = refs[-1]
    started = []
    for i, (src, dst) in enumerate(zip(refs[:half], refs[half:-1])):
        started.append(pltpu.make_async_copy(src, dst, sems.at[i]))
        started[-1].start()
    for copy in started:
        copy.wait()


def on_device(tokens, cotangent, w_query, w_key, w_value, w_out, gain_query, gain_key, lengths):
    vmem = pl.BlockSpec(memory_space=pltpu.VMEM)
    smem = pl.BlockSpec(memory_space=pltpu.SMEM)
    anywhere = pl.BlockSpec(memory_space=pl.ANY)
    shape = jax.ShapeDtypeStruct
    dma = pltpu.SemaphoreType.DMA
    results = [
        shape((TOK, D), BF),
        shape((TOK, D), BF),
        *[shape((WR, H), F32)] * 4,
        shape((2, H), F32),
    ]
    out = pl.pallas_call(
        kernel,
        name="sublayer",
        out_shape=results,
        in_specs=[smem] + [anywhere] * 2 + [vmem] * 6,
        out_specs=[anywhere] * 2 + [vmem] * 5,
        scratch_shapes=[
            pltpu.VMEM((TOK, D), BF),
            pltpu.VMEM((TOK, D), BF),
            pltpu.VMEM((D, 2 * H), BF),
            pltpu.VMEM((D, 2 * H), BF),
            pltpu.VMEM((TOK, 2 * H), F32),
            pltpu.VMEM((TOK, H), F32),
            pltpu.VMEM((TOK, H), F32),
            pltpu.VMEM((NB * TOK, 2 * H), BF),
            pltpu.VMEM((TOK, H), BF),
            pltpu.VMEM((TOK, H), BF),
            pltpu.VMEM((TOK, H), BF),
            pltpu.VMEM((TOK, 3 * H), BF),
            pltpu.VMEM((NP, 2 * TOK, TOK), F32),
            pltpu.VMEM((NP, 2 * TOK, TOK), F32),
            pltpu.VMEM((H, TOK), F32),
            pltpu.VMEM((H, TOK), F32),
            pltpu.VMEM((NP, 2 * TOK, 2 * H), F32),
            pltpu.VMEM((TOK, 2 * H), F32),
            pltpu.VMEM((2, TOK, D), F32),
            pltpu.VMEM((NP, 2 * WR, 4 * H), F32),
            pltpu.VMEM((WR, 4 * H), F32),
            pltpu.VMEM((TOK, D), BF),
            pltpu.VMEM((TOK, D), BF),
            pltpu.VMEM((9, 8, H), F32),
            pltpu.VMEM((8, 8, H), F32),
            pltpu.VMEM((16, TOK, 2 * H), BF),
            pltpu.VMEM((16, TOK, 2 * H), BF),
            pltpu.VMEM((16, WR, 4 * H), BF),
            pltpu.VMEM((16, WR, 4 * H), BF),
            *[b for cols, mode in ATT + TOKENS for b in lane_buffers(cols, mode)],
            dma((6 + len(ATT + TOKENS),)),
            *[dma((20,))] * 3,
            dma((8,)),
            dma((2,)),
            *[dma((30 if mode == "whole" else 48,)) for _, mode in ATT + TOKENS],
        ],
        compiler_params=pltpu.CompilerParams(
            collective_id=0, has_side_effects=True, vmem_limit_bytes=60 * 2**20
        ),
        cost_estimate=pl.CostEstimate(flops=9 * 10**9, bytes_accessed=8 * 2**20, transcendentals=10**6),
    )(
        lengths, tokens, cotangent, w_query, w_key, w_value, w_out,
        gain_query.reshape(1, H), gain_key.reshape(1, H),
    )
    out = pl.pallas_call(
        copies,
        name="results",
        out_shape=results,
        in_specs=[vmem] * 7,
        out_specs=[anywhere] * 7,
        scratch_shapes=[dma((7,))],
    )(*out)
    return tuple(out)


def solution(mesh):
    placed = (
        P("ctx", None),
        P("ctx", None),
        P("ctx", "fsdp"),
        P("ctx", "fsdp"),
        P("ctx", "fsdp"),
        P("ctx", "fsdp"),
        P(),
        P(),
        P(),
    )
    return jax.shard_map(
        on_device,
        mesh=mesh,
        in_specs=placed,
        out_specs=(
            P("ctx", None),
            P("ctx", None),
            P("ctx", "fsdp"),
            P("ctx", "fsdp"),
            P("ctx", "fsdp"),
            P("ctx", "fsdp"),
            P(),
        ),
        check_vma=False,
    )
```

```python
import math

import jax
import jax.numpy as jnp
from jax import lax
from jax.experimental import pallas as pl
from jax.experimental.pallas import tpu as pltpu
from jax.sharding import PartitionSpec as P

EPS = 1e-06
MESH = pl.DeviceIdType.MESH
BF = jnp.bfloat16
F32 = jnp.float32

TOK = 256
D = 3072
H = 128
WR = 192
NB = 16
NP = 8

OWN, YN, XL, XR, XLY, XRY, OPP, OPPY = range(8)


def nt(a, b):
    return lax.dot_general(a, b, (((1,), (1,)), ((), ())), preferred_element_type=F32)


def tn(a, b):
    return lax.dot_general(a, b, (((0,), (0,)), ((), ())), preferred_element_type=F32)


def nn(a, b):
    return jnp.dot(a, b, preferred_element_type=F32)


class Place:
    def __init__(self):
        c = lax.axis_index("ctx")
        f = lax.axis_index("fsdp")
        self.c, self.f = c, f
        y, x, k = c // 8, (c // 2) % 4, c % 2
        yh, z = f // 8, f % 8
        self.k, self.z, self.y_hi = k, z, yh

        def at(y, x, k, yh, z):
            return ((y * 4 + x) * 2 + k, yh * 8 + z)

        xl, xr, xo = (x + 3) % 4, (x + 1) % 4, (x + 2) % 4
        self.sib = at(y, x, 1 - k, yh, z)
        self.xl = at(y, xl, k, yh, z)
        self.xr = at(y, xr, k, yh, z)
        self.xo = at(y, xo, k, yh, z)
        self.x1 = at(y, x + 1 - 2 * (x % 2), k, yh, z)
        self.yn = at(1 - y, x, k, yh, z)
        self.yh = at(y, x, k, 1 - yh, z)
        self.zl = at(y, x, k, yh, (z + 7) % 8)
        self.zr = at(y, x, k, yh, (z + 1) % 8)
        self.z1 = at(y, x, k, yh, z + 1 - 2 * (z % 2))
        self.z2 = at(y, x, k, yh, (z // 4) * 4 + (z + 2) % 4)
        self.z4 = at(y, x, k, yh, (z + 4) % 8)
        self.all = (
            self.sib, self.xl, self.xr, self.xo, self.yn,
            self.yh, self.zl, self.zr, self.z2, self.z4,
        )
        n = 1 - y
        self.chip = (
            y * 4 + x, n * 4 + x, y * 4 + xl, y * 4 + xr,
            n * 4 + xl, n * 4 + xr, y * 4 + xo, n * 4 + xo,
        )


class Link:
    def __init__(self, send, recv):
        self.send, self.recv, self.sent = send, recv, {}

    def copy(self, m, src, dst, to):
        return pltpu.make_async_remote_copy(
            src_ref=src,
            dst_ref=dst,
            send_sem=self.send,
            recv_sem=self.recv.at[m],
            device_id=to,
            device_id_type=MESH,
        )

    def start(self, m, src, dst, to):
        self.sent[m] = self.copy(m, src, dst, to)
        self.sent[m].start()

    def arrived(self, m):
        self.sent[m].wait_recv()

    def drain(self, sized, to):
        self.copy(0, sized, sized, to).wait_send()


def gather(pc, full, rows, link):
    half = rows // 2
    lo, hi = (0, half), (half, half)
    whole = (0, rows)

    def push(m, t, to, part=whole):
        start = pl.multiple_of(pc.chip[t] * (2 * rows) + pc.k * rows + part[0], 16)
        ref = full.at[pl.ds(start, part[1]), :]
        link.start(m, ref, ref, to)

    def share(t):
        push(11 + t, t, pc.sib)

    push(0, OWN, pc.yn)
    push(1, OWN, pc.xl, hi)
    push(2, OWN, pc.xr, lo)
    push(3, OWN, pc.xl, lo)
    push(4, OWN, pc.xr, hi)
    share(OWN)
    yield ()
    link.arrived(1)
    push(7, XR, pc.xl, hi)
    link.arrived(2)
    push(8, XL, pc.xr, lo)
    yield ()
    link.arrived(0)
    push(5, YN, pc.xl)
    push(6, YN, pc.xr)
    share(YN)
    link.arrived(11 + OWN)
    yield (OWN,)
    link.arrived(3)
    share(XR)
    link.arrived(4)
    share(XL)
    link.arrived(11 + YN)
    yield (YN,)
    link.arrived(8)
    push(9, OPP, pc.yn, lo)
    link.arrived(7)
    push(10, OPP, pc.yn, hi)
    share(OPP)
    link.arrived(11 + XR)
    link.arrived(11 + XL)
    yield (XR, XL)
    link.arrived(5)
    share(XRY)
    link.arrived(6)
    share(XLY)
    link.arrived(11 + OPP)
    yield (OPP,)
    link.arrived(9)
    push(18, OPPY, pc.sib, lo)
    link.arrived(10)
    push(19, OPPY, pc.sib, hi)
    link.arrived(11 + XRY)
    link.arrived(11 + XLY)
    yield (XRY, XLY)
    link.arrived(18)
    link.arrived(19)
    yield (OPPY,)
    link.drain(full.at[pl.ds(0, 15 * rows), :], pc.sib)


def scatter(pc, make, part, own, rows, link, sbuf, rbuf):
    half = rows // 2
    lo, hi, whole = pl.ds(0, half), pl.ds(half, half), pl.ds(0, rows)
    mine = pl.multiple_of(pc.k * rows, rows)
    theirs = pl.multiple_of((1 - pc.k) * rows, rows)

    def made(t):
        make(t)
        sbuf[8 + t] = part[t, pl.ds(theirs, rows), :].astype(BF)
        link.start(11 + t, sbuf.at[8 + t], rbuf.at[8 + t], pc.sib)

    def chip_sum(t):
        link.arrived(11 + t)
        part[t, pl.ds(mine, rows), :] += rbuf[8 + t].astype(F32)

    def add(t, slot, m, rows_of=whole):
        link.arrived(m)
        span = pl.ds(pl.multiple_of(mine + rows_of.start, half), rows_of.size)
        part[t, span, :] += rbuf[slot, rows_of, :].astype(F32)

    def push(m, t, slot, to, rows_of=whole):
        span = pl.ds(pl.multiple_of(mine + rows_of.start, half), rows_of.size)
        sbuf[slot, rows_of, :] = part[t, span, :].astype(BF)
        link.start(m, sbuf.at[slot, rows_of], rbuf.at[slot, rows_of], to)

    made(OPPY)
    made(OPP)
    yield
    chip_sum(OPPY)
    push(0, OPPY, 0, pc.yn, lo)
    push(1, OPPY, 0, pc.yn, hi)
    made(XLY)
    made(XRY)
    yield
    chip_sum(XLY)
    push(2, XLY, 1, pc.xl)
    chip_sum(XRY)
    push(3, XRY, 2, pc.xr)
    made(YN)
    made(XL)
    yield
    made(XR)
    chip_sum(OPP)
    add(OPP, 0, 0, lo)
    push(4, OPP, 3, pc.xl, lo)
    add(OPP, 0, 1, hi)
    push(5, OPP, 3, pc.xr, hi)
    yield
    chip_sum(YN)
    add(YN, 1, 2)
    add(YN, 2, 3)
    push(10, YN, 7, pc.yn)
    yield
    chip_sum(XL)
    push(6, XL, 5, pc.xl, hi)
    chip_sum(XR)
    push(7, XR, 6, pc.xr, lo)
    made(OWN)
    yield
    add(XL, 3, 4, lo)
    push(8, XL, 5, pc.xl, lo)
    add(XR, 3, 5, hi)
    push(9, XR, 6, pc.xr, hi)
    yield
    chip_sum(OWN)
    for m in (6, 7, 8, 9, 10):
        link.arrived(m)
    own[...] = part[OWN, pl.ds(mine, rows), :] + (
        rbuf[5].astype(F32) + rbuf[6].astype(F32) + rbuf[7].astype(F32)
    )
    yield
    link.drain(sbuf.at[pl.ds(0, 15)], pc.sib)


SUB = 16
ATT = (((0, D), "halves"),)
TOKENS = (((0, 1024), "whole"), ((1024, 1024), "whole"), ((2048, 1024), "whole"))


ORDER_OF_SUMS = "wzgwzawzgawzwzgzwzgzaagwzz" + "azgw" * 14


def lane_buffers(cols, mode):
    width = cols[1]
    if mode != "across":
        return [pltpu.VMEM((16, SUB, width), BF)] * 2
    return [pltpu.VMEM((14, SUB, width // 2), BF)] * 2 + [pltpu.VMEM((2, TOK // 2, width // 2), BF)] * 2


RIGHT = ((4, 0), (3, 1), (3, 0), (2, 1), (2, 0), (1, 1), (1, 0))
LEFT = ((4, 1), (3, 0), (3, 1), (2, 0), (2, 1), (1, 0), (1, 1))


def sum_heads(pc, cols, mode, term, out, link, sbuf, rbuf, sin=None, rin=None):
    first, width = cols
    half = width // 2
    full = pl.ds(first, width)
    halves, across = mode == "halves", mode == "across"
    side_rows = TOK // 2
    mine = pl.ds(pl.multiple_of(pc.y_hi * side_rows, side_rows), side_rows)
    theirs = pl.ds(pl.multiple_of((1 - pc.y_hi) * side_rows, side_rows), side_rows)

    def at(chip, u):
        if across:
            start = pl.multiple_of(pc.y_hi * side_rows + chip * SUB, SUB)
            return pl.ds(start, SUB), pl.ds(first + u * half, half)
        return pl.ds(pl.multiple_of(chip * (2 * SUB) + u * SUB, SUB), SUB), full

    def piece(chip, u):
        if not halves:
            return at(chip, u)
        start = pl.multiple_of(chip * (2 * SUB) + pc.y_hi * SUB, SUB)
        return pl.ds(start, SUB), pl.ds(first + u * half, half)

    def owner(distance):
        return (pc.z + 8 + distance) % 8

    if across:
        for u in (0, 1):
            sin[u] = term[theirs, pl.ds(first + u * half, half)].astype(BF)
            link.start(46 + u, sin.at[u], rin.at[u], pc.yh)
        yield
        for u in (0, 1):
            link.arrived(46 + u)
            term[mine, pl.ds(first + u * half, half)] += rin[u].astype(F32)
    right = {m: i for i, m in enumerate(RIGHT)}
    left = {m: 7 + i for i, m in enumerate(LEFT)}
    for i in range(7):
        for side, sign, steps, to in ((right, 1, RIGHT, pc.zr), (left, -1, LEFT, pc.zl)):
            d, u = steps[i]
            value = term[at(owner(sign * d), u)]
            before = side.get((d + 1, u))
            if before is not None:
                link.arrived(before)
                value = value + rbuf[before].astype(F32)
            m = side[(d, u)]
            sbuf[m] = value.astype(BF)
            link.start(m, sbuf.at[m], rbuf.at[m], to)
        yield

    def total(u):
        value = term[at(pc.z, u)]
        for m in (right[(1, u)], left[(1, u)]):
            link.arrived(m)
            value = value + rbuf[m].astype(F32)
        return value.astype(BF)

    def forward(m, chip, u, to):
        ref = out.at[piece(chip, u)]
        link.start(m, ref, ref, to)

    def spread(u):
        forward(16 + u, pc.z, u, pc.zr)
        forward(23 + u, pc.z, u, pc.zl)
        if halves or across:
            forward(30 + u, pc.z, u, pc.yh)

    for u in (0, 1):
        if across:
            out[at(pc.z, u)] = total(u)
            spread(u)
            yield
            continue
        sbuf[14 + u] = total(u)
        if not halves:
            link.start(14 + u, sbuf.at[14 + u], rbuf.at[14 + u], pc.yh)
        elif u == 1:
            link.start(14, sbuf.at[14 + 1 - pc.y_hi], rbuf.at[14], pc.yh)
        yield
    for u in () if across else (0, 1):
        if not halves:
            link.arrived(14 + u)
            both = sbuf[14 + u].astype(F32) + rbuf[14 + u].astype(F32)
            out[at(pc.z, u)] = both.astype(BF)
        elif u == 0:
            link.arrived(14)
            both = sbuf[14 + pc.y_hi].astype(F32) + rbuf[14].astype(F32)
            out[at(pc.z, pc.y_hi)] = both.astype(BF)
        spread(u)
        yield

    def hop_id(base, hop, u):
        return base + (2 * (hop - 1) + u if hop < 4 else 6)

    extra = 32
    for hop in (1, 2, 3, 4):
        for u in (0, 1):
            for base, sign, to, last in ((16, -1, pc.zr, 0), (23, 1, pc.zl, 1)):
                if hop == 4 and u != last:
                    continue
                link.arrived(hop_id(base, hop, u))
                if hop < 3 or (hop == 3 and u == last):
                    forward(hop_id(base, hop + 1, u), owner(sign * hop), u, to)
                if halves or across:
                    forward(extra, owner(sign * hop), u, pc.yh)
                    extra += 1
            yield
    if halves or across:
        for m in range(30, extra):
            link.arrived(m)
    link.drain(term.at[pl.ds(0, 15 * SUB), full], pc.zr)


def sum_small(pc, value_ref, link, rbuf):
    for m, to in enumerate((pc.sib, pc.x1, pc.xo, pc.yn, pc.z1, pc.z2, pc.z4, pc.yh)):
        link.start(m, value_ref.at[m], rbuf.at[m], to)
        yield "sent"
        link.arrived(m)
        value_ref[m + 1] = value_ref[m] + rbuf[m]
    link.drain(value_ref.at[pl.ds(0, 8)], pc.sib)


def inv_rms(values):
    return lax.rsqrt(jnp.mean(values * values, -1, keepdims=True) + EPS)


def norm_back(grad, unit, rms, gain):
    scaled = grad * gain
    return rms * (scaled - unit * jnp.mean(scaled * unit, -1, keepdims=True))


def kernel(
    length_ref, tokens_in, cotangent_in, w_query, w_key, w_value, w_out, gain_query, gain_key,
    attended, grad_tokens, g_query, g_key, g_value, g_out, g_gains,
    tokens, cotangent, wkv, wqo, kvp, qp, gacc, kvfull, qn, gb, mixed, dc, probs, gprobs, oacc, qacc,
    dkv, dkv_own, term, wpart, w_own, att_v, tok_v,
    gain_v, gain_r, s_dkv, r_dkv, s_w, r_w, *rest,
):
    lanes, rest = [], list(rest)
    for cols, mode in ATT + TOKENS:
        n = len(lane_buffers(cols, mode))
        lanes.append(rest[:n])
        del rest[:n]
    sent, r_kv, r_qo, r_keys, r_gain, local, *r_lanes = rest
    pc = Place()
    inv_root = 1.0 / math.sqrt(H)
    length = length_ref[0]

    barrier = pltpu.get_barrier_semaphore()
    for other in pc.all:
        pl.semaphore_signal(barrier, inc=1, device_id=other, device_id_type=MESH)
    load_t = pltpu.make_async_copy(tokens_in, tokens, local.at[0])
    load_t.start()
    load_c = pltpu.make_async_copy(cotangent_in, cotangent, local.at[1])
    load_c.start()

    own_rows = pl.ds(pl.multiple_of(pc.c * WR, WR), WR)
    for full, left, right in ((wkv, w_key, w_value), (wqo, w_query, w_out)):
        full[own_rows, 0:H] = left[...]
        full[own_rows, H : 2 * H] = right[...]
    for total in (kvp, qp, gacc, oacc, qacc, gain_v):
        total[...] = jnp.zeros_like(total)
    pl.semaphore_wait(barrier, len(pc.all))

    def model_rows(t):
        return pl.ds(pl.multiple_of(pc.chip[t] * (2 * WR), 2 * WR), 2 * WR)

    def key_rows(t):
        return pl.ds(pl.multiple_of(pc.chip[t] * (2 * TOK), 2 * TOK), 2 * TOK)

    def unit_of(values):
        rms = inv_rms(values)
        return values * rms, rms

    def step(work, n=1):
        for _ in range(n):
            next(work, None)

    def each(works):
        for work in works:
            step(work)

    def project_kv(chips):
        for t in chips:
            r = model_rows(t)
            kvp[...] += nn(tokens[:, r], wkv[r, :])

    def project_qo(chips):
        for t in chips:
            r = model_rows(t)
            qp[...] += nn(tokens[:, r], wqo[r, 0:H])
            gacc[...] += nn(cotangent[:, r], wqo[r, H : 2 * H])

    def run(work, use, n):
        for _ in range(n):
            use(next(work, ()))

    gain_q, gain_k = gain_query[...], gain_key[...]
    first = gather(pc, wkv, WR, Link(sent.at[0], r_kv))
    second = gather(pc, wqo, WR, Link(sent.at[1], r_qo))
    step(first, 2)
    load_t.wait()
    load_c.wait()
    run(first, project_kv, 3)
    step(second)
    run(first, project_kv, 1)
    step(second)
    run(second, project_qo, 1)
    run(first, project_kv, 2)
    run(second, project_qo, 1)
    own_keys = pl.ds(pl.multiple_of(pc.c * TOK, TOK), TOK)
    kvfull[own_keys, 0:H] = (unit_of(kvp[:, 0:H])[0] * gain_k).astype(BF)
    kvfull[own_keys, H : 2 * H] = kvp[:, H : 2 * H].astype(BF)
    third = gather(pc, kvfull, TOK, Link(sent.at[2], r_keys))
    step(third)
    run(second, project_qo, 2)
    step(third)
    run(second, project_qo, 2)
    step(first)
    step(second)
    qn[...] = (unit_of(qp[...])[0] * gain_q).astype(BF)
    gb[...] = gacc[...].astype(BF)

    denom = jnp.zeros((1, TOK), F32)
    for chips in third:
        for t in chips:
            keys, values = kvfull[key_rows(t), 0:H], kvfull[key_rows(t), H : 2 * H]
            scores = nt(keys, qn[...]) * inv_root
            place = pc.chip[t] * (2 * TOK) + lax.broadcasted_iota(jnp.int32, scores.shape, 0)
            weights = jnp.where(place < length, jnp.exp(scores), 0.0)
            probs[t] = weights
            denom = denom + jnp.sum(weights, 0, keepdims=True)
            oacc[...] += tn(values, weights.astype(BF))
            gprobs[t] = nt(values, gb[...])

    inv_denom = 1.0 / denom
    mixed_t = oacc[...] / denom
    mixed[...] = mixed_t.T.astype(BF)
    delta = jnp.sum(gb[...].astype(F32).T * mixed_t.astype(BF).astype(F32), 0, keepdims=True)

    term[0] = nt(mixed[...], wqo[:, H : 2 * H])
    def sums(config, start, src, dst):
        return [
            sum_heads(pc, *config[i], src, dst, Link(sent.at[6 + n], r_lanes[n]), *lanes[n])
            for i, n in enumerate(range(start, start + len(config)))
        ]

    att = sums(ATT, 0, term.at[0], att_v)
    each(att)

    def keys_back(t):
        keys = kvfull[key_rows(t), 0:H]
        probs_t = probs[t] * inv_denom
        scores_b = (probs_t * (gprobs[t] - delta)).astype(BF)
        qacc[...] += tn(keys, scores_b)
        dkv[t, :, 0:H] = nn(scores_b, qn[...]) * inv_root
        dkv[t, :, H : 2 * H] = nn(probs_t.astype(BF), gb[...])

    for i, _ in enumerate(scatter(pc, keys_back, dkv, dkv_own, TOK, Link(sent.at[3], r_kv), s_dkv, r_dkv)):
        if 0 < i < 7:
            each(att)

    grad_qn = qacc[...].T * inv_root
    grad_kn = dkv_own[:, 0:H]
    unit_q, rms_q = unit_of(qp[...])
    unit_k, rms_k = unit_of(kvp[:, 0:H])
    dc[:, 0:H] = norm_back(grad_qn, unit_q, rms_q, gain_q).astype(BF)
    dc[:, H : 2 * H] = norm_back(grad_kn, unit_k, rms_k, gain_k).astype(BF)
    dc[:, 2 * H : 3 * H] = dkv_own[:, H : 2 * H].astype(BF)

    term[1] = nt(dc[:, 0:H], wqo[:, 0:H]) + nt(dc[:, H : 3 * H], wkv[...])
    tok = sums(TOKENS, len(ATT), term.at[1], tok_v)
    step(tok[0])

    gain_v[0, 0:1, :] = jnp.sum(grad_qn * unit_q, 0, keepdims=True)
    gain_v[0, 1:2, :] = jnp.sum(grad_kn * unit_k, 0, keepdims=True)
    gains = sum_small(pc, gain_v, Link(sent.at[5], r_gain), gain_r)

    def weights_back(t):
        r = model_rows(t)
        wpart[t, :, 0 : 3 * H] = tn(tokens[:, r], dc[...])
        wpart[t, :, 3 * H : 4 * H] = tn(cotangent[:, r], mixed[...])

    grads = scatter(pc, weights_back, wpart, w_own, WR, Link(sent.at[4], r_qo), s_w, r_w)
    works = {"w": [grads], "g": [gains], "a": att, "z": tok}
    for name in ORDER_OF_SUMS:
        each(works[name])
    save_a = pltpu.make_async_copy(att_v, attended, local.at[0])
    save_a.start()
    for i, g in enumerate((g_query, g_key, g_value, g_out)):
        g[...] = w_own[:, i * H : (i + 1) * H]
    g_gains[...] = gain_v[8, 0:2, :]
    save_t = pltpu.make_async_copy(tok_v, grad_tokens, local.at[1])
    save_t.start()
    save_a.wait()
    save_t.wait()


def copies(*refs):
    n = (len(refs) - 2) // 3
    sources, targets, through = refs[:n], refs[n : 2 * n], refs[2 * n : 3 * n]
    arrive, leave = refs[3 * n :]
    parts = []
    for src, dst, mid in zip(sources, targets, through):
        rows = src.shape[0]
        size = rows // 2 if rows == TOK else rows
        for start in range(0, rows, size):
            i, span = len(parts), pl.ds(start, size)
            load = pltpu.make_async_copy(src.at[span], mid.at[span], arrive.at[i])
            load.start()
            parts.append((load, pltpu.make_async_copy(mid.at[span], dst.at[span], leave.at[i])))
    for load, store in parts:
        load.wait()
        store.start()
    for _, store in parts:
        store.wait()


def on_device(tokens, cotangent, w_query, w_key, w_value, w_out, gain_query, gain_key, lengths):
    vmem = pl.BlockSpec(memory_space=pltpu.VMEM)
    smem = pl.BlockSpec(memory_space=pltpu.SMEM)
    anywhere = pl.BlockSpec(memory_space=pl.ANY)
    shape = jax.ShapeDtypeStruct
    dma = pltpu.SemaphoreType.DMA
    results = [
        shape((TOK, D), BF),
        shape((TOK, D), BF),
        *[shape((WR, H), F32)] * 4,
        shape((2, H), F32),
    ]
    out = pl.pallas_call(
        kernel,
        name="sublayer",
        out_shape=results,
        in_specs=[smem] + [anywhere] * 2 + [vmem] * 6,
        out_specs=[anywhere] * 2 + [vmem] * 5,
        scratch_shapes=[
            pltpu.VMEM((TOK, D), BF),
            pltpu.VMEM((TOK, D), BF),
            pltpu.VMEM((D, 2 * H), BF),
            pltpu.VMEM((D, 2 * H), BF),
            pltpu.VMEM((TOK, 2 * H), F32),
            pltpu.VMEM((TOK, H), F32),
            pltpu.VMEM((TOK, H), F32),
            pltpu.VMEM((NB * TOK, 2 * H), BF),
            pltpu.VMEM((TOK, H), BF),
            pltpu.VMEM((TOK, H), BF),
            pltpu.VMEM((TOK, H), BF),
            pltpu.VMEM((TOK, 3 * H), BF),
            pltpu.VMEM((NP, 2 * TOK, TOK), F32),
            pltpu.VMEM((NP, 2 * TOK, TOK), F32),
            pltpu.VMEM((H, TOK), F32),
            pltpu.VMEM((H, TOK), F32),
            pltpu.VMEM((NP, 2 * TOK, 2 * H), F32),
            pltpu.VMEM((TOK, 2 * H), F32),
            pltpu.VMEM((2, TOK, D), F32),
            pltpu.VMEM((NP, 2 * WR, 4 * H), F32),
            pltpu.VMEM((WR, 4 * H), F32),
            pltpu.VMEM((TOK, D), BF),
            pltpu.VMEM((TOK, D), BF),
            pltpu.VMEM((9, 8, H), F32),
            pltpu.VMEM((8, 8, H), F32),
            pltpu.VMEM((16, TOK, 2 * H), BF),
            pltpu.VMEM((16, TOK, 2 * H), BF),
            pltpu.VMEM((16, WR, 4 * H), BF),
            pltpu.VMEM((16, WR, 4 * H), BF),
            *[b for cols, mode in ATT + TOKENS for b in lane_buffers(cols, mode)],
            dma((6 + len(ATT + TOKENS),)),
            *[dma((20,))] * 3,
            dma((8,)),
            dma((2,)),
            *[dma((30 if mode == "whole" else 48,)) for _, mode in ATT + TOKENS],
        ],
        compiler_params=pltpu.CompilerParams(
            collective_id=0, has_side_effects=True, vmem_limit_bytes=60 * 2**20
        ),
        cost_estimate=pl.CostEstimate(flops=9 * 10**9, bytes_accessed=8 * 2**20, transcendentals=10**6),
    )(
        lengths, tokens, cotangent, w_query, w_key, w_value, w_out,
        gain_query.reshape(1, H), gain_key.reshape(1, H),
    )
    out = pl.pallas_call(
        copies,
        name="results",
        out_shape=results,
        in_specs=[anywhere] * 7,
        out_specs=[anywhere] * 7,
        scratch_shapes=[*[pltpu.VMEM(r.shape, r.dtype) for r in results], dma((9,)), dma((9,))],
    )(*out)
    return tuple(out)


def solution(mesh):
    placed = (
        P("ctx", None),
        P("ctx", None),
        P("ctx", "fsdp"),
        P("ctx", "fsdp"),
        P("ctx", "fsdp"),
        P("ctx", "fsdp"),
        P(),
        P(),
        P(),
    )
    return jax.shard_map(
        on_device,
        mesh=mesh,
        in_specs=placed,
        out_specs=(
            P("ctx", None),
            P("ctx", None),
            P("ctx", "fsdp"),
            P("ctx", "fsdp"),
            P("ctx", "fsdp"),
            P("ctx", "fsdp"),
            P(),
        ),
        check_vma=False,
    )
```

```python
import math

import jax
import jax.numpy as jnp
from jax import lax
from jax.experimental import pallas as pl
from jax.experimental.pallas import tpu as pltpu
from jax.sharding import PartitionSpec as P

EPS = 1e-06
MESH = pl.DeviceIdType.MESH
BF = jnp.bfloat16
F32 = jnp.float32

TOK = 256
D = 3072
H = 128
WR = 192
NB = 16
NP = 8

OWN, YN, XL, XR, XLY, XRY, OPP, OPPY = range(8)


def nt(a, b):
    return lax.dot_general(a, b, (((1,), (1,)), ((), ())), preferred_element_type=F32)


def tn(a, b):
    return lax.dot_general(a, b, (((0,), (0,)), ((), ())), preferred_element_type=F32)


def nn(a, b):
    return jnp.dot(a, b, preferred_element_type=F32)


class Place:
    def __init__(self):
        c = lax.axis_index("ctx")
        f = lax.axis_index("fsdp")
        self.c, self.f = c, f
        y, x, k = c // 8, (c // 2) % 4, c % 2
        yh, z = f // 8, f % 8
        self.k, self.z, self.y_hi = k, z, yh

        def at(y, x, k, yh, z):
            return ((y * 4 + x) * 2 + k, yh * 8 + z)

        xl, xr, xo = (x + 3) % 4, (x + 1) % 4, (x + 2) % 4
        self.sib = at(y, x, 1 - k, yh, z)
        self.xl = at(y, xl, k, yh, z)
        self.xr = at(y, xr, k, yh, z)
        self.xo = at(y, xo, k, yh, z)
        self.x1 = at(y, x + 1 - 2 * (x % 2), k, yh, z)
        self.yn = at(1 - y, x, k, yh, z)
        self.yh = at(y, x, k, 1 - yh, z)
        self.zl = at(y, x, k, yh, (z + 7) % 8)
        self.zr = at(y, x, k, yh, (z + 1) % 8)
        self.z1 = at(y, x, k, yh, z + 1 - 2 * (z % 2))
        self.z2 = at(y, x, k, yh, (z // 4) * 4 + (z + 2) % 4)
        self.z4 = at(y, x, k, yh, (z + 4) % 8)
        self.all = (
            self.sib, self.xl, self.xr, self.xo, self.yn,
            self.yh, self.zl, self.zr, self.z2, self.z4,
        )
        n = 1 - y
        self.chip = (
            y * 4 + x, n * 4 + x, y * 4 + xl, y * 4 + xr,
            n * 4 + xl, n * 4 + xr, y * 4 + xo, n * 4 + xo,
        )


class Link:
    def __init__(self, send, recv):
        self.send, self.recv, self.sent = send, recv, {}

    def copy(self, m, src, dst, to):
        return pltpu.make_async_remote_copy(
            src_ref=src,
            dst_ref=dst,
            send_sem=self.send,
            recv_sem=self.recv.at[m],
            device_id=to,
            device_id_type=MESH,
        )

    def start(self, m, src, dst, to):
        self.sent[m] = self.copy(m, src, dst, to)
        self.sent[m].start()

    def arrived(self, m):
        self.sent[m].wait_recv()

    def drain(self, sized, to):
        self.copy(0, sized, sized, to).wait_send()


def gather(pc, full, rows, link):
    half = rows // 2
    lo, hi = (0, half), (half, half)
    whole = (0, rows)

    def push(m, t, to, part=whole):
        start = pl.multiple_of(pc.chip[t] * (2 * rows) + pc.k * rows + part[0], 16)
        ref = full.at[pl.ds(start, part[1]), :]
        link.start(m, ref, ref, to)

    def share(t):
        push(11 + t, t, pc.sib)

    push(0, OWN, pc.yn)
    push(1, OWN, pc.xl, hi)
    push(2, OWN, pc.xr, lo)
    push(3, OWN, pc.xl, lo)
    push(4, OWN, pc.xr, hi)
    share(OWN)
    yield ()
    link.arrived(1)
    push(7, XR, pc.xl, hi)
    link.arrived(2)
    push(8, XL, pc.xr, lo)
    yield ()
    link.arrived(0)
    push(5, YN, pc.xl)
    push(6, YN, pc.xr)
    share(YN)
    link.arrived(11 + OWN)
    yield (OWN,)
    link.arrived(3)
    share(XR)
    link.arrived(4)
    share(XL)
    link.arrived(11 + YN)
    yield (YN,)
    link.arrived(8)
    push(9, OPP, pc.yn, lo)
    link.arrived(7)
    push(10, OPP, pc.yn, hi)
    share(OPP)
    link.arrived(11 + XR)
    link.arrived(11 + XL)
    yield (XR, XL)
    link.arrived(5)
    share(XRY)
    link.arrived(6)
    share(XLY)
    link.arrived(11 + OPP)
    yield (OPP,)
    link.arrived(9)
    push(18, OPPY, pc.sib, lo)
    link.arrived(10)
    push(19, OPPY, pc.sib, hi)
    link.arrived(11 + XRY)
    link.arrived(11 + XLY)
    yield (XRY, XLY)
    link.arrived(18)
    link.arrived(19)
    yield (OPPY,)
    link.drain(full.at[pl.ds(0, 15 * rows), :], pc.sib)


def scatter(pc, make, part, own, rows, link, sbuf, rbuf):
    half = rows // 2
    lo, hi, whole = pl.ds(0, half), pl.ds(half, half), pl.ds(0, rows)
    mine = pl.multiple_of(pc.k * rows, rows)
    theirs = pl.multiple_of((1 - pc.k) * rows, rows)

    def made(t):
        make(t)
        sbuf[8 + t] = part[t, pl.ds(theirs, rows), :].astype(BF)
        link.start(11 + t, sbuf.at[8 + t], rbuf.at[8 + t], pc.sib)

    def chip_sum(t):
        link.arrived(11 + t)
        part[t, pl.ds(mine, rows), :] += rbuf[8 + t].astype(F32)

    def add(t, slot, m, rows_of=whole):
        link.arrived(m)
        span = pl.ds(pl.multiple_of(mine + rows_of.start, half), rows_of.size)
        part[t, span, :] += rbuf[slot, rows_of, :].astype(F32)

    def push(m, t, slot, to, rows_of=whole):
        span = pl.ds(pl.multiple_of(mine + rows_of.start, half), rows_of.size)
        sbuf[slot, rows_of, :] = part[t, span, :].astype(BF)
        link.start(m, sbuf.at[slot, rows_of], rbuf.at[slot, rows_of], to)

    made(OPPY)
    made(OPP)
    yield
    chip_sum(OPPY)
    push(0, OPPY, 0, pc.yn, lo)
    push(1, OPPY, 0, pc.yn, hi)
    made(XLY)
    made(XRY)
    yield
    chip_sum(XLY)
    push(2, XLY, 1, pc.xl)
    chip_sum(XRY)
    push(3, XRY, 2, pc.xr)
    made(YN)
    made(XL)
    yield
    made(XR)
    chip_sum(OPP)
    add(OPP, 0, 0, lo)
    push(4, OPP, 3, pc.xl, lo)
    add(OPP, 0, 1, hi)
    push(5, OPP, 3, pc.xr, hi)
    yield
    chip_sum(YN)
    add(YN, 1, 2)
    add(YN, 2, 3)
    push(10, YN, 7, pc.yn)
    yield
    chip_sum(XL)
    push(6, XL, 5, pc.xl, hi)
    chip_sum(XR)
    push(7, XR, 6, pc.xr, lo)
    made(OWN)
    yield
    add(XL, 3, 4, lo)
    push(8, XL, 5, pc.xl, lo)
    add(XR, 3, 5, hi)
    push(9, XR, 6, pc.xr, hi)
    yield
    chip_sum(OWN)
    for m in (6, 7, 8, 9, 10):
        link.arrived(m)
    own[...] = part[OWN, pl.ds(mine, rows), :] + (
        rbuf[5].astype(F32) + rbuf[6].astype(F32) + rbuf[7].astype(F32)
    )
    yield
    link.drain(sbuf.at[pl.ds(0, 15)], pc.sib)


SUB = 16
ATT = (((0, D), "halves"),)
TOKENS = (((0, 1024), "whole"), ((1024, 1024), "whole"), ((2048, 1024), "whole"))


ORDER_OF_SUMS = "wzgwzawzgawzgwzgzwzgzgaagwzzg" + "azgw" * 14


def lane_buffers(cols, mode):
    width = cols[1]
    if mode != "across":
        return [pltpu.VMEM((16, SUB, width), BF)] * 2
    return [pltpu.VMEM((14, SUB, width // 2), BF)] * 2 + [pltpu.VMEM((2, TOK // 2, width // 2), BF)] * 2


RIGHT = ((4, 0), (3, 1), (3, 0), (2, 1), (2, 0), (1, 1), (1, 0))
LEFT = ((4, 1), (3, 0), (3, 1), (2, 0), (2, 1), (1, 0), (1, 1))


def sum_heads(pc, cols, mode, term, out, link, sbuf, rbuf, sin=None, rin=None):
    first, width = cols
    half = width // 2
    full = pl.ds(first, width)
    halves, across = mode == "halves", mode == "across"
    side_rows = TOK // 2
    mine = pl.ds(pl.multiple_of(pc.y_hi * side_rows, side_rows), side_rows)
    theirs = pl.ds(pl.multiple_of((1 - pc.y_hi) * side_rows, side_rows), side_rows)

    def at(chip, u):
        if across:
            start = pl.multiple_of(pc.y_hi * side_rows + chip * SUB, SUB)
            return pl.ds(start, SUB), pl.ds(first + u * half, half)
        return pl.ds(pl.multiple_of(chip * (2 * SUB) + u * SUB, SUB), SUB), full

    def piece(chip, u):
        if not halves:
            return at(chip, u)
        start = pl.multiple_of(chip * (2 * SUB) + pc.y_hi * SUB, SUB)
        return pl.ds(start, SUB), pl.ds(first + u * half, half)

    def owner(distance):
        return (pc.z + 8 + distance) % 8

    if across:
        for u in (0, 1):
            sin[u] = term[theirs, pl.ds(first + u * half, half)].astype(BF)
            link.start(46 + u, sin.at[u], rin.at[u], pc.yh)
        yield
        for u in (0, 1):
            link.arrived(46 + u)
            term[mine, pl.ds(first + u * half, half)] += rin[u].astype(F32)
    right = {m: i for i, m in enumerate(RIGHT)}
    left = {m: 7 + i for i, m in enumerate(LEFT)}
    for i in range(7):
        for side, sign, steps, to in ((right, 1, RIGHT, pc.zr), (left, -1, LEFT, pc.zl)):
            d, u = steps[i]
            value = term[at(owner(sign * d), u)]
            before = side.get((d + 1, u))
            if before is not None:
                link.arrived(before)
                value = value + rbuf[before].astype(F32)
            m = side[(d, u)]
            sbuf[m] = value.astype(BF)
            link.start(m, sbuf.at[m], rbuf.at[m], to)
        yield

    def total(u):
        value = term[at(pc.z, u)]
        for m in (right[(1, u)], left[(1, u)]):
            link.arrived(m)
            value = value + rbuf[m].astype(F32)
        return value.astype(BF)

    def forward(m, chip, u, to):
        ref = out.at[piece(chip, u)]
        link.start(m, ref, ref, to)

    def spread(u):
        forward(16 + u, pc.z, u, pc.zr)
        forward(23 + u, pc.z, u, pc.zl)
        if halves or across:
            forward(30 + u, pc.z, u, pc.yh)

    for u in (0, 1):
        if across:
            out[at(pc.z, u)] = total(u)
            spread(u)
            yield
            continue
        sbuf[14 + u] = total(u)
        if not halves:
            link.start(14 + u, sbuf.at[14 + u], rbuf.at[14 + u], pc.yh)
        elif u == 1:
            link.start(14, sbuf.at[14 + 1 - pc.y_hi], rbuf.at[14], pc.yh)
        yield
    for u in () if across else (0, 1):
        if not halves:
            link.arrived(14 + u)
            both = sbuf[14 + u].astype(F32) + rbuf[14 + u].astype(F32)
            out[at(pc.z, u)] = both.astype(BF)
        elif u == 0:
            link.arrived(14)
            both = sbuf[14 + pc.y_hi].astype(F32) + rbuf[14].astype(F32)
            out[at(pc.z, pc.y_hi)] = both.astype(BF)
        spread(u)
        yield

    def hop_id(base, hop, u):
        return base + (2 * (hop - 1) + u if hop < 4 else 6)

    extra = 32
    for hop in (1, 2, 3, 4):
        for u in (0, 1):
            for base, sign, to, last in ((16, -1, pc.zr, 0), (23, 1, pc.zl, 1)):
                if hop == 4 and u != last:
                    continue
                link.arrived(hop_id(base, hop, u))
                if hop < 3 or (hop == 3 and u == last):
                    forward(hop_id(base, hop + 1, u), owner(sign * hop), u, to)
                if halves or across:
                    forward(extra, owner(sign * hop), u, pc.yh)
                    extra += 1
            yield
    if halves or across:
        for m in range(30, extra):
            link.arrived(m)
    link.drain(term.at[pl.ds(0, 15 * SUB), full], pc.zr)


def sum_small(pc, value_ref, link, rbuf):
    for m, to in enumerate((pc.sib, pc.x1, pc.xo, pc.yn, pc.z1, pc.z2, pc.z4, pc.yh)):
        link.start(m, value_ref.at[m], rbuf.at[m], to)
        yield "sent"
        link.arrived(m)
        value_ref[m + 1] = value_ref[m] + rbuf[m]
    link.drain(value_ref.at[pl.ds(0, 8)], pc.sib)


def inv_rms(values):
    return lax.rsqrt(jnp.mean(values * values, -1, keepdims=True) + EPS)


def norm_back(grad, unit, rms, gain):
    scaled = grad * gain
    return rms * (scaled - unit * jnp.mean(scaled * unit, -1, keepdims=True))


def kernel(
    length_ref, tokens_in, cotangent_in, w_query, w_key, w_value, w_out, gain_query, gain_key,
    attended, grad_tokens, g_query, g_key, g_value, g_out, g_gains,
    tokens, cotangent, wkv, wqo, kvp, qp, gacc, kvfull, qn, gb, mixed, dc, probs, gprobs, oacc, qacc,
    dkv, dkv_own, term, wpart, w_own, att_v, tok_v,
    gain_v, gain_r, s_dkv, r_dkv, s_w, r_w, *rest,
):
    lanes, rest = [], list(rest)
    for cols, mode in ATT + TOKENS:
        n = len(lane_buffers(cols, mode))
        lanes.append(rest[:n])
        del rest[:n]
    sent, r_kv, r_qo, r_keys, r_gain, local, *r_lanes = rest
    pc = Place()
    inv_root = 1.0 / math.sqrt(H)
    length = length_ref[0]

    barrier = pltpu.get_barrier_semaphore()
    for other in pc.all:
        pl.semaphore_signal(barrier, inc=1, device_id=other, device_id_type=MESH)
    load_t = pltpu.make_async_copy(tokens_in, tokens, local.at[0])
    load_t.start()
    load_c = pltpu.make_async_copy(cotangent_in, cotangent, local.at[1])
    load_c.start()

    own_rows = pl.ds(pl.multiple_of(pc.c * WR, WR), WR)
    for full, left, right in ((wkv, w_key, w_value), (wqo, w_query, w_out)):
        full[own_rows, 0:H] = left[...]
        full[own_rows, H : 2 * H] = right[...]
    for total in (kvp, qp, gacc, oacc, qacc, gain_v):
        total[...] = jnp.zeros_like(total)
    pl.semaphore_wait(barrier, len(pc.all))

    def model_rows(t):
        return pl.ds(pl.multiple_of(pc.chip[t] * (2 * WR), 2 * WR), 2 * WR)

    def key_rows(t):
        return pl.ds(pl.multiple_of(pc.chip[t] * (2 * TOK), 2 * TOK), 2 * TOK)

    def unit_of(values):
        rms = inv_rms(values)
        return values * rms, rms

    def step(work, n=1):
        for _ in range(n):
            next(work, None)

    def each(works):
        for work in works:
            step(work)

    def project_kv(chips):
        for t in chips:
            r = model_rows(t)
            kvp[...] += nn(tokens[:, r], wkv[r, :])

    def project_qo(chips):
        for t in chips:
            r = model_rows(t)
            qp[...] += nn(tokens[:, r], wqo[r, 0:H])
            gacc[...] += nn(cotangent[:, r], wqo[r, H : 2 * H])

    def run(work, use, n):
        for _ in range(n):
            use(next(work, ()))

    gain_q, gain_k = gain_query[...], gain_key[...]
    first = gather(pc, wkv, WR, Link(sent.at[0], r_kv))
    second = gather(pc, wqo, WR, Link(sent.at[1], r_qo))
    step(first, 2)
    load_t.wait()
    load_c.wait()
    run(first, project_kv, 3)
    step(second)
    run(first, project_kv, 1)
    step(second)
    run(second, project_qo, 1)
    run(first, project_kv, 2)
    run(second, project_qo, 1)
    own_keys = pl.ds(pl.multiple_of(pc.c * TOK, TOK), TOK)
    kvfull[own_keys, 0:H] = (unit_of(kvp[:, 0:H])[0] * gain_k).astype(BF)
    kvfull[own_keys, H : 2 * H] = kvp[:, H : 2 * H].astype(BF)
    third = gather(pc, kvfull, TOK, Link(sent.at[2], r_keys))
    step(third)
    run(second, project_qo, 2)
    step(third)
    run(second, project_qo, 2)
    step(first)
    step(second)
    qn[...] = (unit_of(qp[...])[0] * gain_q).astype(BF)
    gb[...] = gacc[...].astype(BF)

    denom = jnp.zeros((1, TOK), F32)
    for chips in third:
        for t in chips:
            keys, values = kvfull[key_rows(t), 0:H], kvfull[key_rows(t), H : 2 * H]
            scores = nt(keys, qn[...]) * inv_root
            place = pc.chip[t] * (2 * TOK) + lax.broadcasted_iota(jnp.int32, scores.shape, 0)
            weights = jnp.where(place < length, jnp.exp(scores), 0.0)
            probs[t] = weights
            denom = denom + jnp.sum(weights, 0, keepdims=True)
            oacc[...] += tn(values, weights.astype(BF))
            gprobs[t] = nt(values, gb[...])

    inv_denom = 1.0 / denom
    mixed_t = oacc[...] / denom
    mixed[...] = mixed_t.T.astype(BF)
    delta = jnp.sum(gb[...].astype(F32).T * mixed_t.astype(BF).astype(F32), 0, keepdims=True)

    term[0] = nt(mixed[...], wqo[:, H : 2 * H])
    def sums(config, start, src, dst):
        return [
            sum_heads(pc, *config[i], src, dst, Link(sent.at[6 + n], r_lanes[n]), *lanes[n])
            for i, n in enumerate(range(start, start + len(config)))
        ]

    att = sums(ATT, 0, term.at[0], att_v)
    each(att)

    def keys_back(t):
        keys = kvfull[key_rows(t), 0:H]
        probs_t = probs[t] * inv_denom
        scores_b = (probs_t * (gprobs[t] - delta)).astype(BF)
        qacc[...] += tn(keys, scores_b)
        dkv[t, :, 0:H] = nn(scores_b, qn[...]) * inv_root
        dkv[t, :, H : 2 * H] = nn(probs_t.astype(BF), gb[...])

    for i, _ in enumerate(scatter(pc, keys_back, dkv, dkv_own, TOK, Link(sent.at[3], r_kv), s_dkv, r_dkv)):
        if 0 < i < 7:
            each(att)

    grad_qn = qacc[...].T * inv_root
    grad_kn = dkv_own[:, 0:H]
    unit_q, rms_q = unit_of(qp[...])
    unit_k, rms_k = unit_of(kvp[:, 0:H])
    dc[:, 0:H] = norm_back(grad_qn, unit_q, rms_q, gain_q).astype(BF)
    dc[:, H : 2 * H] = norm_back(grad_kn, unit_k, rms_k, gain_k).astype(BF)
    dc[:, 2 * H : 3 * H] = dkv_own[:, H : 2 * H].astype(BF)

    term[1] = nt(dc[:, 0:H], wqo[:, 0:H]) + nt(dc[:, H : 3 * H], wkv[...])
    tok = sums(TOKENS, len(ATT), term.at[1], tok_v)
    step(tok[0])

    gain_v[0, 0:1, :] = jnp.sum(grad_qn * unit_q, 0, keepdims=True)
    gain_v[0, 1:2, :] = jnp.sum(grad_kn * unit_k, 0, keepdims=True)
    gains = sum_small(pc, gain_v, Link(sent.at[5], r_gain), gain_r)

    def weights_back(t):
        r = model_rows(t)
        wpart[t, :, 0 : 3 * H] = tn(tokens[:, r], dc[...])
        wpart[t, :, 3 * H : 4 * H] = tn(cotangent[:, r], mixed[...])

    grads = scatter(pc, weights_back, wpart, w_own, WR, Link(sent.at[4], r_qo), s_w, r_w)
    works = {"w": [grads], "g": [gains], "a": att, "z": tok}
    for name in ORDER_OF_SUMS:
        each(works[name])
    save_a = pltpu.make_async_copy(att_v, attended, local.at[0])
    save_a.start()
    for i, g in enumerate((g_query, g_key, g_value, g_out)):
        g[...] = w_own[:, i * H : (i + 1) * H]
    g_gains[...] = gain_v[8, 0:2, :]
    save_t = pltpu.make_async_copy(tok_v, grad_tokens, local.at[1])
    save_t.start()
    save_a.wait()
    save_t.wait()


def copies(*refs):
    n = (len(refs) - 2) // 3
    sources, targets, through = refs[:n], refs[n : 2 * n], refs[2 * n : 3 * n]
    arrive, leave = refs[3 * n :]
    parts = []
    for src, dst, mid in zip(sources, targets, through):
        rows = src.shape[0]
        size = rows // 2 if rows == TOK else rows
        for start in range(0, rows, size):
            i, span = len(parts), pl.ds(start, size)
            load = pltpu.make_async_copy(src.at[span], mid.at[span], arrive.at[i])
            load.start()
            parts.append((load, pltpu.make_async_copy(mid.at[span], dst.at[span], leave.at[i])))
    for load, store in parts:
        load.wait()
        store.start()
    for _, store in parts:
        store.wait()


def on_device(tokens, cotangent, w_query, w_key, w_value, w_out, gain_query, gain_key, lengths):
    vmem = pl.BlockSpec(memory_space=pltpu.VMEM)
    smem = pl.BlockSpec(memory_space=pltpu.SMEM)
    anywhere = pl.BlockSpec(memory_space=pl.ANY)
    shape = jax.ShapeDtypeStruct
    dma = pltpu.SemaphoreType.DMA
    results = [
        shape((TOK, D), BF),
        shape((TOK, D), BF),
        *[shape((WR, H), F32)] * 4,
        shape((2, H), F32),
    ]
    out = pl.pallas_call(
        kernel,
        name="sublayer",
        out_shape=results,
        in_specs=[smem] + [anywhere] * 2 + [vmem] * 6,
        out_specs=[anywhere] * 2 + [vmem] * 5,
        scratch_shapes=[
            pltpu.VMEM((TOK, D), BF),
            pltpu.VMEM((TOK, D), BF),
            pltpu.VMEM((D, 2 * H), BF),
            pltpu.VMEM((D, 2 * H), BF),
            pltpu.VMEM((TOK, 2 * H), F32),
            pltpu.VMEM((TOK, H), F32),
            pltpu.VMEM((TOK, H), F32),
            pltpu.VMEM((NB * TOK, 2 * H), BF),
            pltpu.VMEM((TOK, H), BF),
            pltpu.VMEM((TOK, H), BF),
            pltpu.VMEM((TOK, H), BF),
            pltpu.VMEM((TOK, 3 * H), BF),
            pltpu.VMEM((NP, 2 * TOK, TOK), F32),
            pltpu.VMEM((NP, 2 * TOK, TOK), F32),
            pltpu.VMEM((H, TOK), F32),
            pltpu.VMEM((H, TOK), F32),
            pltpu.VMEM((NP, 2 * TOK, 2 * H), F32),
            pltpu.VMEM((TOK, 2 * H), F32),
            pltpu.VMEM((2, TOK, D), F32),
            pltpu.VMEM((NP, 2 * WR, 4 * H), F32),
            pltpu.VMEM((WR, 4 * H), F32),
            pltpu.VMEM((TOK, D), BF),
            pltpu.VMEM((TOK, D), BF),
            pltpu.VMEM((9, 8, H), F32),
            pltpu.VMEM((8, 8, H), F32),
            pltpu.VMEM((16, TOK, 2 * H), BF),
            pltpu.VMEM((16, TOK, 2 * H), BF),
            pltpu.VMEM((16, WR, 4 * H), BF),
            pltpu.VMEM((16, WR, 4 * H), BF),
            *[b for cols, mode in ATT + TOKENS for b in lane_buffers(cols, mode)],
            dma((6 + len(ATT + TOKENS),)),
            *[dma((20,))] * 3,
            dma((8,)),
            dma((2,)),
            *[dma((30 if mode == "whole" else 48,)) for _, mode in ATT + TOKENS],
        ],
        compiler_params=pltpu.CompilerParams(
            collective_id=0, has_side_effects=True, vmem_limit_bytes=60 * 2**20
        ),
        cost_estimate=pl.CostEstimate(flops=9 * 10**9, bytes_accessed=8 * 2**20, transcendentals=10**6),
    )(
        lengths, tokens, cotangent, w_query, w_key, w_value, w_out,
        gain_query.reshape(1, H), gain_key.reshape(1, H),
    )
    out = pl.pallas_call(
        copies,
        name="results",
        out_shape=results,
        in_specs=[anywhere] * 7,
        out_specs=[anywhere] * 7,
        scratch_shapes=[*[pltpu.VMEM(r.shape, r.dtype) for r in results], dma((9,)), dma((9,))],
    )(*out)
    return tuple(out)


def solution(mesh):
    placed = (
        P("ctx", None),
        P("ctx", None),
        P("ctx", "fsdp"),
        P("ctx", "fsdp"),
        P("ctx", "fsdp"),
        P("ctx", "fsdp"),
        P(),
        P(),
        P(),
    )
    return jax.shard_map(
        on_device,
        mesh=mesh,
        in_specs=placed,
        out_specs=(
            P("ctx", None),
            P("ctx", None),
            P("ctx", "fsdp"),
            P("ctx", "fsdp"),
            P("ctx", "fsdp"),
            P("ctx", "fsdp"),
            P(),
        ),
        check_vma=False,
    )
```
